512 devices in a mesh: dp: 4 (over x), section: 32 (over z, core), tensor: 4 (over y).
Axes of the slice: x: 4, y: 4, z: 16, core: 2. Of those that a mesh axis runs over, the one named last changes fastest.
Arguments:
- hidden: bfloat16 [512, 8192], P('dp', ('section', 'tensor'))
- weight: bfloat16 [8192, 65536], P('dp', ('section', 'tensor'))
- labels: int32 [512], P('dp'), may hold values from 0 to 65535
- counts: int32 [4, 65536], P('dp', ('section', 'tensor')), may hold values from 0 to 1023, as said below
Outputs:
- grad_weight: bfloat16 [8192, 65536], P('dp', ('section', 'tensor'))
- grad_hidden_t: bfloat16 [8192, 512], P(('dp', 'section', 'tensor'))
- loss: float32 [4], P('dp')
The draws below stay inside these ranges and needn't reach their ends.
Inputs may be any that keep to these rules, and one draw needn't show every extreme that they name: counts of replica r lie in 0 to 256 * (r + 1) - 1, and each replica reaches its largest value at some entry.
All inputs are finite; a program needn't handle non-finite values.
Results may differ from the reference program's by a relative error of at most 0.006.
Values may be sent and summed in bfloat16 or wider, within the bound.
A program may use at most 64 MiB of HBM per device.

```python
import jax
import jax.numpy as jnp
from jax import lax

D = 8192
BATCH = 128
VOCAB = 65536
TOKENS = 512
N_DP = 4


aligned_count = 8


def drawn_columns(key):
    pick_key = jax.random.fold_in(key, 101)
    value_key = jax.random.fold_in(key, 102)
    step_key = jax.random.fold_in(key, 103)
    first_pick = jax.random.randint(pick_key, (aligned_count,), 0, VOCAB)
    second_pick = (first_pick + jax.random.randint(step_key, (aligned_count,), 1, VOCAB)) % VOCAB
    raw_values = jax.random.normal(value_key, (aligned_count, 2, D), jnp.float32)
    aligned = raw_values * lax.rsqrt(jnp.mean(raw_values * raw_values, axis=2, keepdims=True)) * (3.0 * D ** (-0.5))
    return (first_pick, second_pick, aligned)


def draw_weight(key, part):
    first_pick, second_pick, aligned = drawn_columns(key)
    key = jax.random.fold_in(key, 7)
    base_key, scale_key = jax.random.split(key)
    spread = jnp.exp(jax.random.uniform(scale_key, (1, VOCAB), jnp.float32, jnp.log(0.5), jnp.log(2.0)))
    base_values = jax.random.normal(base_key, (D, VOCAB), jnp.float32)
    matrix = base_values * spread * (3.0 * D ** (-0.5))
    matrix = matrix.at[:, first_pick].set(aligned[:, 0, :].T)
    matrix = matrix.at[:, second_pick].set(aligned[:, 1, :].T)
    return matrix.astype(jnp.bfloat16)


def draw_hidden(key, part):
    key = jax.random.fold_in(key, 9)
    value_key = jax.random.fold_in(key, 0)
    values = jax.random.normal(value_key, (TOKENS, D), jnp.float32)
    return values.astype(jnp.bfloat16)


def draw_counts(key, part):
    key = jax.random.fold_in(key, 5)
    value_key, top_key, low_key = jax.random.split(key, 3)
    upper_limit = 256 * (1 + jnp.arange(N_DP, dtype=jnp.int32))[:, None]
    values = jax.random.randint(value_key, (N_DP, VOCAB), 0, upper_limit, jnp.int32)
    top_column = jax.random.randint(top_key, (N_DP, 1), 0, VOCAB, jnp.int32)
    low_column = (top_column + jax.random.randint(low_key, (N_DP, 1), 1, VOCAB, jnp.int32)) % VOCAB
    columns = lax.broadcasted_iota(jnp.int32, (N_DP, VOCAB), 1)
    values = jnp.where(columns == top_column, upper_limit - 1, values)
    values = jnp.where(columns == low_column, 0, values)
    return values


def with_ends(array, key, low, high):
    longest = array.shape.index(max(array.shape))
    spots = []
    for shift in (0, 1):
        where = [jax.random.randint(jax.random.fold_in(key, axis), (), 0, length) for axis, length in enumerate(array.shape)]
        where[longest] = (where[longest] + shift) % array.shape[longest]
        spots.append(tuple(where))
    return array.at[spots[0]].set(low).at[spots[1]].set(high)


def setup_inputs(seed: int = 0) -> dict:
    keys = jax.random.split(jax.random.key(seed), 5)
    return {
        "hidden": draw_hidden(jax.random.fold_in(keys[4], 71), 0),
        "weight": draw_weight(jax.random.fold_in(keys[4], 71), 0),
        "labels": with_ends(jax.random.randint(keys[2], (TOKENS,), 0, VOCAB), jax.random.fold_in(keys[2], 1), 0, VOCAB - 1).astype(jnp.int32),
        "counts": draw_counts(jax.random.fold_in(keys[4], 71), 0),
    }


def replica_pass(hidden_rows, label_rows, weight, factor):
    logits = jnp.dot(hidden_rows, weight, preferred_element_type=jnp.float32)
    row_top = lax.optimization_barrier(jnp.max(logits, axis=1))
    row_total = lax.optimization_barrier(jnp.sum(jnp.exp(logits - row_top[:, None]), axis=1))
    columns = lax.broadcasted_iota(jnp.int32, logits.shape, 1)
    is_label = columns == label_rows[:, None]
    target = lax.optimization_barrier(jnp.sum(jnp.where(is_label, logits, 0.0), axis=1))
    token_weight = factor[label_rows]
    scaled = token_weight / jnp.mean(token_weight)
    loss_value = jnp.sum(scaled * (jnp.log(row_total) + row_top - target)) / label_rows.shape[0]
    softmax_rows = jnp.exp(logits - row_top[:, None]) / row_total[:, None]
    grad_logits = (scaled[:, None] * (softmax_rows - is_label.astype(jnp.float32))).astype(jnp.bfloat16)
    return (grad_logits, loss_value)

def reference(hidden, weight, labels, counts):
    totals = lax.optimization_barrier(jnp.sum(counts, axis=0))
    factor = lax.rsqrt(1.0 + totals.astype(jnp.float32))
    grouped = hidden.reshape(N_DP, BATCH, D)
    label_groups = labels.reshape(N_DP, BATCH)

    def one_replica(inputs):
        return replica_pass(inputs[0], inputs[1], weight, factor)
    grad_logits, losses = lax.map(one_replica, (grouped, label_groups))
    grad_all = grad_logits.reshape(TOKENS, VOCAB)
    grad_weight = lax.dot_general(hidden, grad_all, (((0,), (0,)), ((), ())), preferred_element_type=jnp.float32).astype(jnp.bfloat16)
    grad_hidden_t = lax.dot_general(weight, grad_all, (((1,), (1,)), ((), ())), preferred_element_type=jnp.float32).astype(jnp.bfloat16)
    return (grad_weight, grad_hidden_t, losses)
```

```python
import functools

import jax
import jax.numpy as jnp
from jax import lax
from jax.experimental import pallas as pl
from jax.experimental.pallas import tpu as pltpu
from jax.sharding import PartitionSpec as P

NX, NY, NZ, NC = 4, 4, 16, 2
ZL = NZ // NX
BATCH = 128
FEAT = 64
VL = 512
MESH = pl.DeviceIdType.MESH
BF = jnp.bfloat16
F32 = jnp.float32


def spread(i):
    half = (i + 1) // 2
    return NZ // 2 + (1 - 2 * lax.rem(i, 2)) * half


def kernel(
    hid, w_hbm, lab, cnt,
    gw_hbm, gh_out, loss_out,
    wv, wt, zbuf, ht, part, bufa, bufb, rfl, rfr, cbuf, fcol, ebuf, stz, sty, gt,
    psend, pown, crecv, q, ya, yb, sa, sb, yl, yr, rz, zrb, gwv,
    w_sem, gw_sem,
    az_s, az_r, ax_s, ax_r, ct_s, ct_r, ay_s, ay_r, ac_s, ac_r,
    b_s, b_r, sz_s, sz_r, sy_s, sy_r, d_s, d_r,
    fc_s, fc_r, fy_s, fy_r, fz_s, fz_r,
):
    x = lax.axis_index("dp")
    s = lax.axis_index("section")
    y = lax.axis_index("tensor")
    z, c = s // 2, lax.rem(s, 2)
    zs, zl0 = z // ZL, lax.rem(z, ZL)
    oc = 1 - c

    def xat(k):
        return lax.rem(x + k + NX, NX)

    def yat(k):
        return lax.rem(y + k + NY, NY)

    def zat(k):
        return lax.rem(z + k + NZ, NZ)

    def to_x(k):
        return (xat(k), s, y)

    def to_y(k):
        return (x, s, yat(k))

    def to_z(zz):
        return (x, 2 * zz + c, y)

    def to_q(k):
        j = lax.rem(y * 2 + c + k, 8)
        return (x, 2 * z + lax.rem(j, 2), j // 2)

    sibling = (x, 2 * z + oc, y)
    sends = []

    def rcopy(src, dst, ss, rs, dev):
        return pltpu.make_async_remote_copy(
            src_ref=src, dst_ref=dst, send_sem=ss, recv_sem=rs, device_id=dev, device_id_type=MESH
        )

    def send(src, dst, ss, rs, dev):
        d = rcopy(src, dst, ss, rs, dev)
        d.start()
        sends.append(d)

    def recv(dst, rs):
        rcopy(dst, dst, rs, rs, sibling).wait_recv()

    w_copy = pltpu.make_async_copy(w_hbm, wv, w_sem)
    w_copy.start()

    eye = (lax.broadcasted_iota(jnp.int32, (FEAT, FEAT), 0) == lax.broadcasted_iota(jnp.int32, (FEAT, FEAT), 1))
    zbuf[z] = lax.dot_general(
        eye.astype(F32).astype(BF), hid[...], (((1,), (1,)), ((), ())), preferred_element_type=F32
    ).astype(BF)
    cbuf[x] = cnt[...]

    barrier = pltpu.get_barrier_semaphore()

    def greet_z(k, _):
        pl.semaphore_signal(barrier, inc=1, device_id=to_z(zat(k)), device_id_type=MESH)
        return 0

    lax.fori_loop(1, NZ, greet_z, 0)
    for k in range(1, 8):
        pl.semaphore_signal(barrier, inc=1, device_id=to_q(k), device_id_type=MESH)
    for k in range(1, NX):
        pl.semaphore_signal(barrier, inc=1, device_id=to_x(k), device_id_type=MESH)
    pl.semaphore_wait(barrier, 25)

    def start_z(i, _):
        k = spread(i)
        rcopy(zbuf.at[z], zbuf.at[z], az_s.at[k], az_r.at[k], to_z(zat(k))).start()
        return 0

    lax.fori_loop(0, NZ - 1, start_z, 0)
    for k in range(1, NX):
        send(cbuf.at[x], cbuf.at[x], ct_s.at[k], ct_r.at[k], to_x(k))

    w_copy.wait()

    def turn(i, _):
        rows = wv[pl.ds(2 * i, 2)].reshape(256, VL)
        wt[:, pl.ds(pl.multiple_of(i * 256, 256), 256)] = rows.T
        return 0

    lax.fori_loop(0, 8, turn, 0)
    for k in range(1, NX):
        recv(cbuf.at[xat(-k)], ct_r.at[k])
    totals = cbuf[0] + cbuf[1] + cbuf[2] + cbuf[3]
    factor = lax.rsqrt(1.0 + totals.astype(F32))
    fcol[...] = jnp.broadcast_to(factor, (BATCH, VL)).T

    def wait_z(k, _):
        recv(zbuf.at[zat(-k)], az_r.at[k])
        return 0

    lax.fori_loop(1, NZ, wait_z, 0)

    for k in (2, 1, 3):
        to = xat(k)
        send(zbuf.at[pl.ds(ZL * to, ZL)], ht.at[x, :, c, y], ax_s.at[k], ax_r.at[k], to_x(k))
    ht[x, :, c, y] = zbuf[pl.ds(ZL * x, ZL)]

    def hid_y(k):
        r = xat(-k)
        if k:
            recv(ht.at[r, :, c, y], ax_r.at[k])
        for d, e in ((0, 1), (1, -1)):
            send(ht.at[r, :, c, y], ht.at[r, :, c, y], ay_s.at[k, d], ay_r.at[k, d], to_y(e))

    def hid_relay(k):
        r = xat(-k)
        for d, e in ((0, 1), (1, -1)):
            recv(ht.at[r, :, c, yat(-e)], ay_r.at[k, d])
            half = pl.ds(2 * d, 2)
            ref = ht.at[r, half, c, yat(-e)]
            send(ref, ref, ay_s.at[k, 2 + d], ay_r.at[k, 2 + d], to_y(e))

    def hid_core(k):
        r = xat(-k)
        for d in (0, 1):
            recv(ht.at[r, pl.ds(2 * d, 2), c, yat(2)], ay_r.at[k, 2 + d])
        send(ht.at[r, :, c], ht.at[r, :, c], ac_s.at[k], ac_r.at[k], sibling)

    def logits_of(k):
        r = xat(-k)
        recv(ht.at[r, :, oc], ac_r.at[k])

        def tile(i, _):
            rows = pl.ds(pl.multiple_of(i * 256, 256), 256)
            part[r, rows] = jnp.dot(wt[rows, :], ht[r].reshape(2048, BATCH), preferred_element_type=F32)
            return 0

        lax.fori_loop(0, 2, tile, 0)
        top, low = pl.ds(0, 256), pl.ds(256, 256)
        if k == 2:
            send(part.at[r, top], bufa, b_s.at[0], b_r.at[0], to_x(1))
            send(part.at[r, low], bufb, b_s.at[1], b_r.at[1], to_x(-1))
        if k == 3:
            send(part.at[r, low], rfl.at[low], b_s.at[2], b_r.at[2], to_x(1))
            recv(bufa, b_r.at[0])
            part[r, top] = part[r, top] + bufa[...]
            send(part.at[r, top], rfl.at[top], b_s.at[3], b_r.at[3], to_x(1))
        if k == 1:
            send(part.at[r, top], rfr.at[top], b_s.at[4], b_r.at[4], to_x(-1))
            recv(bufb, b_r.at[1])
            part[r, low] = part[r, low] + bufb[...]
            send(part.at[r, low], rfr.at[low], b_s.at[5], b_r.at[5], to_x(-1))

    stages = (hid_y, hid_relay, hid_core, logits_of)
    order = (2, 1, 3, 0)
    for t in range(len(order) + len(stages) - 1):
        for j, stage in enumerate(stages):
            if 0 <= t - j < len(order):
                stage(order[t - j])

    top, low = pl.ds(0, 256), pl.ds(256, 256)
    recv(rfl.at[low], b_r.at[2])
    recv(rfl.at[top], b_r.at[3])
    recv(rfr.at[top], b_r.at[4])
    recv(rfr.at[low], b_r.at[5])

    logits = part[x] + rfl[...] + rfr[...]
    ids = lax.broadcasted_iota(jnp.int32, (VL, BATCH), 0) + (s * NY + y) * VL
    hit = ids == lab[...]
    m0 = jnp.max(logits, axis=0, keepdims=True)
    e0 = jnp.exp(logits - m0)
    ebuf[...] = e0
    zero = jnp.zeros((4, BATCH), F32)
    stz[z] = jnp.concatenate(
        [
            m0,
            jnp.sum(e0, axis=0, keepdims=True),
            jnp.sum(jnp.where(hit, logits, 0.0), axis=0, keepdims=True),
            jnp.sum(jnp.where(hit, fcol[...], 0.0), axis=0, keepdims=True),
            zero,
        ],
        axis=0,
    )

    def combine(ref):
        v = ref[...]
        tops = v[:, 0:1, :]
        m = jnp.max(tops, axis=0)
        t = jnp.sum(v[:, 1:2, :] * jnp.exp(tops - m[None]), axis=0)
        return m, t, jnp.sum(v[:, 2:3, :], axis=0), jnp.sum(v[:, 3:4, :], axis=0)

    def start_sz(i, _):
        k = spread(i)
        rcopy(stz.at[z], stz.at[z], sz_s.at[k], sz_r.at[k], to_z(zat(k))).start()
        return 0

    def wait_sz(k, _):
        recv(stz.at[zat(-k)], sz_r.at[k])
        return 0

    lax.fori_loop(0, NZ - 1, start_sz, 0)
    lax.fori_loop(1, NZ, wait_sz, 0)
    me = y * 2 + c
    sty[me] = jnp.concatenate([*combine(stz), zero], axis=0)
    for k in range(1, 8):
        send(sty.at[me], sty.at[me], sy_s.at[k], sy_r.at[k], to_q(k))
    for k in range(1, 8):
        recv(sty.at[lax.rem(me - k + 8, 8)], sy_r.at[k])
    m, total, target, weight = combine(sty)
    scaled = weight / jnp.mean(weight)
    loss_out[0] = jnp.sum(scaled * (jnp.log(total) + m - target)) / BATCH
    rate = jnp.exp(m0 - m) / total
    gt[x] = (scaled * (ebuf[...] * rate - hit.astype(F32))).astype(BF)

    for d, e in ((0, 1), (1, -1)):
        send(gt.at[x], gt.at[x], d_s.at[d], d_r.at[d], to_x(e))
    for d, e in ((0, 1), (1, -1)):
        recv(gt.at[xat(-e)], d_r.at[d])
        ref = gt.at[xat(-e), pl.ds(256 * d, 256)]
        send(ref, ref, d_s.at[2 + d], d_r.at[2 + d], to_x(e))
    for d in (0, 1):
        recv(gt.at[xat(2), pl.ds(256 * d, 256)], d_r.at[2 + d])

    def gall():
        return jnp.concatenate([gt[r] for r in range(NX)], axis=1)

    def gh_dot(k):
        zz = lax.rem(zs + k, NX)
        rows = wv[pl.ds(ZL * zz, ZL), oc].reshape(256, VL)
        psend[zz] = jnp.dot(rows, gall(), preferred_element_type=F32).astype(BF).reshape(ZL, NY, 16, 512)
        send(psend.at[zz], crecv.at[zz], fc_s.at[k], fc_r.at[k], sibling)
        rows = wv[pl.ds(ZL * zz, ZL), c].reshape(256, VL)
        pown[zz] = jnp.dot(rows, gall(), preferred_element_type=F32).reshape(ZL, NY, 16, 512)

    def gh_core(k):
        zz = lax.rem(zs + k, NX)
        recv(crecv.at[zz], fc_r.at[k])
        q[zz] = (pown[zz] + crecv[zz].astype(F32)).astype(BF)
        up, down = pl.ds(0, 2), pl.ds(2, 2)
        send(q.at[zz, up, yat(2)], ya.at[k], fy_s.at[k, 0], fy_r.at[k, 0], to_y(1))
        send(q.at[zz, down, yat(2)], yb.at[k], fy_s.at[k, 1], fy_r.at[k, 1], to_y(-1))
        send(q.at[zz, down, yat(1)], yl.at[k, down], fy_s.at[k, 2], fy_r.at[k, 2], to_y(1))
        send(q.at[zz, up, yat(-1)], yr.at[k, up], fy_s.at[k, 3], fy_r.at[k, 3], to_y(-1))

    def gh_relay(k):
        zz = lax.rem(zs + k, NX)
        up, down = pl.ds(0, 2), pl.ds(2, 2)
        recv(ya.at[k], fy_r.at[k, 0])
        sa[k] = (q[zz, up, yat(1)].astype(F32) + ya[k].astype(F32)).astype(BF)
        send(sa.at[k], yl.at[k, up], fy_s.at[k, 4], fy_r.at[k, 4], to_y(1))
        recv(yb.at[k], fy_r.at[k, 1])
        sb[k] = (q[zz, down, yat(-1)].astype(F32) + yb[k].astype(F32)).astype(BF)
        send(sb.at[k], yr.at[k, down], fy_s.at[k, 5], fy_r.at[k, 5], to_y(-1))

    def gh_z(k):
        zz = lax.rem(zs + k, NX)
        up, down = pl.ds(0, 2), pl.ds(2, 2)
        recv(yl.at[k, down], fy_r.at[k, 2])
        recv(yr.at[k, up], fy_r.at[k, 3])
        recv(yl.at[k, up], fy_r.at[k, 4])
        recv(yr.at[k, down], fy_r.at[k, 5])
        rz[zz] = (q[zz, :, y].astype(F32) + yl[k].astype(F32) + yr[k].astype(F32)).astype(BF)
        for j in range(0 if k else 1, ZL):
            l = lax.rem(zl0 + j, ZL)
            send(rz.at[zz, l], zrb.at[z], fz_s.at[k, j], fz_r.at[z], to_z(ZL * zz + l))

    stages = (gh_dot, gh_core, gh_relay, gh_z)
    order = (2, 1, 3, 0)
    for t in range(len(order) + len(stages) - 1):
        for j, stage in enumerate(stages):
            if 0 <= t - j < len(order):
                stage(order[t - j])

    def gw_tile(i, _):
        lhs = jnp.concatenate([ht[r, i // 2, lax.rem(i, 2)].reshape(256, BATCH) for r in range(NX)], axis=1)
        gwv[i] = lax.dot_general(lhs, gall(), (((1,), (1,)), ((), ())), preferred_element_type=F32).astype(BF)
        pltpu.make_async_copy(gwv.at[i], gw_hbm.at[i], gw_sem.at[i]).start()
        return 0

    lax.fori_loop(0, 8, gw_tile, 0)

    zrb[z] = rz[zs, zl0]

    def wait_fz(k, _):
        recv(zrb.at[zat(-k)], fz_r.at[zat(-k)])
        return 0

    lax.fori_loop(1, NZ, wait_fz, 0)
    gh_out[...] = jnp.sum(zrb[...].astype(F32), axis=0).astype(BF)

    def gw_wait(i, _):
        pltpu.make_async_copy(gwv.at[i], gw_hbm.at[i], gw_sem.at[i]).wait()
        return 0

    lax.fori_loop(0, 8, gw_wait, 0)

    def done_z(k, _):
        rcopy(zbuf.at[z], zbuf.at[z], az_s.at[k], az_r.at[k], sibling).wait_send()
        rcopy(stz.at[z], stz.at[z], sz_s.at[k], sz_r.at[k], sibling).wait_send()
        return 0

    lax.fori_loop(1, NZ, done_z, 0)
    for d in sends:
        d.wait_send()


def body(hidden, weight, labels, counts):
    dma = pltpu.SemaphoreType.DMA
    v = pltpu.VMEM
    scratch = [
        v((16, 2, 64, VL), BF),
        v((VL, 2048), BF),
        v((NZ, FEAT, BATCH), BF),
        v((NX, ZL, NC, NY, FEAT, BATCH), BF),
        v((NX, VL, BATCH), F32),
        v((256, BATCH), F32),
        v((256, BATCH), F32),
        v((VL, BATCH), F32),
        v((VL, BATCH), F32),
        v((NX, 1, VL), jnp.int32),
        v((VL, BATCH), F32),
        v((VL, BATCH), F32),
        v((NZ, 8, BATCH), F32),
        v((8, 8, BATCH), F32),
        v((NX, VL, BATCH), BF),
        v((NX, ZL, NY, 16, 512), BF),
        v((NX, ZL, NY, 16, 512), F32),
        v((NX, ZL, NY, 16, 512), BF),
        v((NX, ZL, NY, 16, 512), BF),
        v((NX, 2, 16, 512), BF),
        v((NX, 2, 16, 512), BF),
        v((NX, 2, 16, 512), BF),
        v((NX, 2, 16, 512), BF),
        v((NX, ZL, 16, 512), BF),
        v((NX, ZL, 16, 512), BF),
        v((NX, ZL, 16, 512), BF),
        v((NZ, 16, 512), BF),
        v((8, 256, VL), BF),
        dma, dma((8,)),
        dma((16,)), dma((16,)), dma((4,)), dma((4,)), dma((4,)), dma((4,)),
        dma((4, 4)), dma((4, 4)), dma((4,)), dma((4,)),
        dma((6,)), dma((6,)), dma((16,)), dma((16,)), dma((8,)), dma((8,)), dma((4,)), dma((4,)),
        dma((4,)), dma((4,)), dma((4, 6)), dma((4, 6)), dma((4, 4)), dma((16,)),
    ]
    vmem = pl.BlockSpec(memory_space=pltpu.VMEM)
    hbm = pl.BlockSpec(memory_space=pl.ANY)
    gw, gh, loss = pl.pallas_call(
        kernel,
        out_shape=(
            jax.ShapeDtypeStruct((8, 256, VL), BF),
            jax.ShapeDtypeStruct((16, 512), BF),
            jax.ShapeDtypeStruct((1,), F32),
        ),
        in_specs=[vmem, hbm, vmem, vmem],
        out_specs=(hbm, vmem, pl.BlockSpec(memory_space=pltpu.SMEM)),
        scratch_shapes=scratch,
        compiler_params=pltpu.CompilerParams(
            collective_id=0, has_side_effects=True, vmem_limit_bytes=48 * 1024 * 1024
        ),
        cost_estimate=pl.CostEstimate(flops=3 * 2**30, bytes_accessed=2**22, transcendentals=2**16),
    )(hidden, weight.reshape(16, 2, 64, VL), labels.reshape(1, BATCH), counts)
    return gw.reshape(2048, VL), gh, loss


def solution(mesh):
    in_specs = (
        P("dp", ("section", "tensor")),
        P("dp", ("section", "tensor")),
        P("dp"),
        P("dp", ("section", "tensor")),
    )
    out_specs = (P("dp", ("section", "tensor")), P(("dp", "section", "tensor"), None), P("dp"))
    return jax.shard_map(body, mesh=mesh, in_specs=in_specs, out_specs=out_specs, check_vma=False)
```

```python
import functools

import jax
import jax.numpy as jnp
from jax import lax
from jax.experimental import pallas as pl
from jax.experimental.pallas import tpu as pltpu
from jax.sharding import PartitionSpec as P

NX, NY, NZ, NC = 4, 4, 16, 2
ZL = NZ // NX
BATCH = 128
FEAT = 64
VL = 512
MESH = pl.DeviceIdType.MESH
BF = jnp.bfloat16
F32 = jnp.float32


def spread(i):
    half = (i + 1) // 2
    return NZ // 2 + (1 - 2 * lax.rem(i, 2)) * half


def kernel(
    hid_hbm, w_hbm, lab_hbm, cnt_hbm,
    gw_hbm, gh_out, loss_out,
    wv, wt, zbuf, ht, part, bufa, bufb, rfl, rfr, cbuf, lbuf, fcol, eb, stz, sty, coef, gall,
    psend, pown, crecv, q, ya, yb, sa, sb, yl, yr, rz, zrb, gwv,
    w_sem, in_sem, gw_sem,
    az_s, az_r, ax_s, ax_r, ct_s, ct_r, lb_s, lb_r, ay_s, ay_r, ac_s, ac_r,
    b_s, b_r, sz_s, sz_r, sy_s, sy_r, eb_s, eb_r, co_s, co_r,
    fc_s, fc_r, fy_s, fy_r, fz_s, fz_r,
):
    x = lax.axis_index("dp")
    s = lax.axis_index("section")
    y = lax.axis_index("tensor")
    z, c = s // 2, lax.rem(s, 2)
    zs, zl0 = z // ZL, lax.rem(z, ZL)
    oc = 1 - c

    def xat(k):
        return lax.rem(x + k + NX, NX)

    def yat(k):
        return lax.rem(y + k + NY, NY)

    def zat(k):
        return lax.rem(z + k + NZ, NZ)

    def to_x(k):
        return (xat(k), s, y)

    def to_y(k):
        return (x, s, yat(k))

    def to_z(zz):
        return (x, 2 * zz + c, y)

    def to_q(k):
        j = lax.rem(y * 2 + c + k, 8)
        return (x, 2 * z + lax.rem(j, 2), j // 2)

    sibling = (x, 2 * z + oc, y)
    sends = []

    def rcopy(src, dst, ss, rs, dev):
        return pltpu.make_async_remote_copy(
            src_ref=src, dst_ref=dst, send_sem=ss, recv_sem=rs, device_id=dev, device_id_type=MESH
        )

    def send(src, dst, ss, rs, dev):
        d = rcopy(src, dst, ss, rs, dev)
        d.start()
        sends.append(d)

    def recv(dst, rs):
        rcopy(dst, dst, rs, rs, sibling).wait_recv()

    w_copy = pltpu.make_async_copy(w_hbm, wv, w_sem)
    ins = [
        pltpu.make_async_copy(hid_hbm, zbuf.at[z], in_sem.at[0]),
        pltpu.make_async_copy(cnt_hbm, cbuf.at[x], in_sem.at[1]),
        pltpu.make_async_copy(lab_hbm, lbuf.at[x], in_sem.at[2]),
    ]
    for copy in ins:
        copy.start()

    barrier = pltpu.get_barrier_semaphore()

    def greet_z(k, _):
        pl.semaphore_signal(barrier, inc=1, device_id=to_z(zat(k)), device_id_type=MESH)
        return 0

    lax.fori_loop(1, NZ, greet_z, 0)
    for k in range(1, 8):
        pl.semaphore_signal(barrier, inc=1, device_id=to_q(k), device_id_type=MESH)
    for k in range(1, NX):
        pl.semaphore_signal(barrier, inc=1, device_id=to_x(k), device_id_type=MESH)
    w_copy.start()
    for copy in ins:
        copy.wait()
    pl.semaphore_wait(barrier, 25)

    def start_z(i, _):
        k = spread(i)
        rcopy(zbuf.at[z], zbuf.at[z], az_s.at[k], az_r.at[k], to_z(zat(k))).start()
        return 0

    lax.fori_loop(0, NZ - 1, start_z, 0)
    for k in range(1, NX):
        send(cbuf.at[x], cbuf.at[x], ct_s.at[k], ct_r.at[k], to_x(k))
        send(lbuf.at[x], lbuf.at[x], lb_s.at[k], lb_r.at[k], to_x(k))

    w_copy.wait()

    def turn(i, _):
        rows = wv[pl.ds(2 * i, 2)].reshape(256, VL)
        wt[:, pl.ds(pl.multiple_of(i * 256, 256), 256)] = rows.T
        return 0

    lax.fori_loop(0, 8, turn, 0)
    for k in range(1, NX):
        recv(cbuf.at[xat(-k)], ct_r.at[k])
        recv(lbuf.at[xat(-k)], lb_r.at[k])
    totals = cbuf[0] + cbuf[1] + cbuf[2] + cbuf[3]
    factor = lax.rsqrt(1.0 + totals.astype(F32))
    fcol[...] = jnp.broadcast_to(factor, (BATCH, VL)).T

    def wait_z(k, _):
        recv(zbuf.at[zat(-k)], az_r.at[k])
        rcopy(zbuf.at[z], zbuf.at[z], az_s.at[k], az_r.at[k], sibling).wait_send()
        return 0

    lax.fori_loop(1, NZ, wait_z, 0)

    for k in (2, 1, 3):
        to = xat(k)
        send(zbuf.at[pl.ds(ZL * to, ZL)], ht.at[x, :, c, y], ax_s.at[k], ax_r.at[k], to_x(k))
    ht[x, :, c, y] = zbuf[pl.ds(ZL * x, ZL)]

    def hid_y(k):
        r = xat(-k)
        if k:
            recv(ht.at[r, :, c, y], ax_r.at[k])
        for d, e in ((0, 1), (1, -1)):
            send(ht.at[r, :, c, y], ht.at[r, :, c, y], ay_s.at[k, d], ay_r.at[k, d], to_y(e))

    def hid_relay(k):
        r = xat(-k)
        for d, e in ((0, 1), (1, -1)):
            recv(ht.at[r, :, c, yat(-e)], ay_r.at[k, d])
            half = pl.ds(2 * d, 2)
            ref = ht.at[r, half, c, yat(-e)]
            send(ref, ref, ay_s.at[k, 2 + d], ay_r.at[k, 2 + d], to_y(e))

    def hid_core(k):
        r = xat(-k)
        for d in (0, 1):
            recv(ht.at[r, pl.ds(2 * d, 2), c, yat(2)], ay_r.at[k, 2 + d])
        send(ht.at[r, :, c], ht.at[r, :, c], ac_s.at[k], ac_r.at[k], sibling)

    def logits_of(k):
        r = xat(-k)
        recv(ht.at[r, :, oc], ac_r.at[k])

        def tile(i, _):
            rows = pl.ds(pl.multiple_of(i * 256, 256), 256)
            part[r, rows] = jnp.dot(wt[rows, :], ht[r].reshape(2048, BATCH), preferred_element_type=F32)
            return 0

        lax.fori_loop(0, 2, tile, 0)
        top, low = pl.ds(0, 256), pl.ds(256, 256)
        if k == 2:
            send(part.at[r, top], bufa, b_s.at[0], b_r.at[0], to_x(1))
            send(part.at[r, low], bufb, b_s.at[1], b_r.at[1], to_x(-1))
        if k == 3:
            send(part.at[r, low], rfl.at[low], b_s.at[2], b_r.at[2], to_x(1))
        if k == 1:
            send(part.at[r, top], rfr.at[top], b_s.at[4], b_r.at[4], to_x(-1))

    def logits_relay(k):
        r = xat(-k)
        top, low = pl.ds(0, 256), pl.ds(256, 256)
        if k == 3:
            recv(bufa, b_r.at[0])
            part[r, top] = part[r, top] + bufa[...]
            send(part.at[r, top], rfl.at[top], b_s.at[3], b_r.at[3], to_x(1))
        if k == 1:
            recv(bufb, b_r.at[1])
            part[r, low] = part[r, low] + bufb[...]
            send(part.at[r, low], rfr.at[low], b_s.at[5], b_r.at[5], to_x(-1))

    for stage, k in (
        (hid_y, 0), (hid_y, 2), (hid_y, 1), (hid_y, 3),
        (hid_relay, 0), (hid_relay, 2), (hid_relay, 1), (hid_relay, 3),
        (hid_core, 2), (hid_core, 1), (logits_of, 2), (hid_core, 3), (logits_of, 1),
        (hid_core, 0), (logits_of, 3), (logits_of, 0), (logits_relay, 3), (logits_relay, 1),
    ):
        stage(k)

    top, low = pl.ds(0, 256), pl.ds(256, 256)
    recv(rfl.at[low], b_r.at[2])
    recv(rfl.at[top], b_r.at[3])
    recv(rfr.at[top], b_r.at[4])
    recv(rfr.at[low], b_r.at[5])

    logits = part[x] + rfl[...] + rfr[...]
    ids = lax.broadcasted_iota(jnp.int32, (VL, BATCH), 0) + (s * NY + y) * VL
    hit = ids == lbuf[x]
    m0 = jnp.max(logits, axis=0, keepdims=True)
    e0 = jnp.exp(logits - m0)
    eb[x] = e0.astype(BF)
    for k in (2, 1, 3):
        send(eb.at[x], eb.at[x], eb_s.at[k], eb_r.at[k], to_x(k))
    zero = jnp.zeros((4, BATCH), F32)
    stz[z] = jnp.concatenate(
        [
            m0,
            jnp.sum(e0, axis=0, keepdims=True),
            jnp.sum(jnp.where(hit, logits, 0.0), axis=0, keepdims=True),
            jnp.sum(jnp.where(hit, fcol[...], 0.0), axis=0, keepdims=True),
            zero,
        ],
        axis=0,
    )

    def combine(ref):
        v = ref[...]
        tops = v[:, 0:1, :]
        m = jnp.max(tops, axis=0)
        t = jnp.sum(v[:, 1:2, :] * jnp.exp(tops - m[None]), axis=0)
        return m, t, jnp.sum(v[:, 2:3, :], axis=0), jnp.sum(v[:, 3:4, :], axis=0)

    def start_sz(i, _):
        k = spread(i)
        rcopy(stz.at[z], stz.at[z], sz_s.at[k], sz_r.at[k], to_z(zat(k))).start()
        return 0

    def wait_sz(k, _):
        recv(stz.at[zat(-k)], sz_r.at[k])
        rcopy(stz.at[z], stz.at[z], sz_s.at[k], sz_r.at[k], sibling).wait_send()
        return 0

    lax.fori_loop(0, NZ - 1, start_sz, 0)
    lax.fori_loop(1, NZ, wait_sz, 0)
    me = y * 2 + c
    sty[me] = jnp.concatenate([*combine(stz), zero], axis=0)
    for k in range(1, 8):
        send(sty.at[me], sty.at[me], sy_s.at[k], sy_r.at[k], to_q(k))
    for k in range(1, 8):
        recv(sty.at[lax.rem(me - k + 8, 8)], sy_r.at[k])
    m, total, target, weight = combine(sty)
    scaled = weight / jnp.mean(weight)
    loss_out[0] = jnp.sum(scaled * (jnp.log(total) + m - target)) / BATCH
    coef[x] = jnp.concatenate([scaled * jnp.exp(m0 - m) / total, scaled, jnp.zeros((6, BATCH), F32)], axis=0)

    for k in (2, 1, 3):
        send(coef.at[x], coef.at[x], co_s.at[k], co_r.at[k], to_x(k))
    for k in (0, 1, 3, 2):
        r = xat(-k)
        if k:
            recv(eb.at[r], eb_r.at[k])
            recv(coef.at[r], co_r.at[k])
        v = coef[r]
        gall[:, pl.ds(pl.multiple_of(r * BATCH, BATCH), BATCH)] = (
            eb[r].astype(F32) * v[0:1] - jnp.where(ids == lbuf[r], v[1:2], 0.0)
        ).astype(BF)
    def gh_dot(k):
        zz = lax.rem(zs + k, NX)
        rows = wv[pl.ds(ZL * zz, ZL), oc].reshape(256, VL)
        psend[zz] = jnp.dot(rows, gall[...], preferred_element_type=F32).astype(BF).reshape(ZL, NY, 16, 512)
        send(psend.at[zz], crecv.at[zz], fc_s.at[k], fc_r.at[k], sibling)

    def gh_own(k):
        zz = lax.rem(zs + k, NX)
        rows = wv[pl.ds(ZL * zz, ZL), c].reshape(256, VL)
        pown[zz] = jnp.dot(rows, gall[...], preferred_element_type=F32).reshape(ZL, NY, 16, 512)

    def gh_core(k):
        zz = lax.rem(zs + k, NX)
        recv(crecv.at[zz], fc_r.at[k])
        q[zz] = (pown[zz] + crecv[zz].astype(F32)).astype(BF)
        up, down = pl.ds(0, 2), pl.ds(2, 2)
        send(q.at[zz, up, yat(2)], ya.at[k], fy_s.at[k, 0], fy_r.at[k, 0], to_y(1))
        send(q.at[zz, down, yat(2)], yb.at[k], fy_s.at[k, 1], fy_r.at[k, 1], to_y(-1))
        send(q.at[zz, down, yat(1)], yl.at[k, down], fy_s.at[k, 2], fy_r.at[k, 2], to_y(1))
        send(q.at[zz, up, yat(-1)], yr.at[k, up], fy_s.at[k, 3], fy_r.at[k, 3], to_y(-1))

    def gh_relay(k):
        zz = lax.rem(zs + k, NX)
        up, down = pl.ds(0, 2), pl.ds(2, 2)
        recv(ya.at[k], fy_r.at[k, 0])
        sa[k] = (q[zz, up, yat(1)].astype(F32) + ya[k].astype(F32)).astype(BF)
        send(sa.at[k], yl.at[k, up], fy_s.at[k, 4], fy_r.at[k, 4], to_y(1))
        recv(yb.at[k], fy_r.at[k, 1])
        sb[k] = (q[zz, down, yat(-1)].astype(F32) + yb[k].astype(F32)).astype(BF)
        send(sb.at[k], yr.at[k, down], fy_s.at[k, 5], fy_r.at[k, 5], to_y(-1))

    def gh_z(k):
        zz = lax.rem(zs + k, NX)
        up, down = pl.ds(0, 2), pl.ds(2, 2)
        recv(yl.at[k, down], fy_r.at[k, 2])
        recv(yr.at[k, up], fy_r.at[k, 3])
        recv(yl.at[k, up], fy_r.at[k, 4])
        recv(yr.at[k, down], fy_r.at[k, 5])
        rz[zz] = (q[zz, :, y].astype(F32) + yl[k].astype(F32) + yr[k].astype(F32)).astype(BF)
        for j in range(0 if k else 1, ZL):
            l = lax.rem(zl0 + j, ZL)
            send(rz.at[zz, l], zrb.at[z], fz_s.at[k, j], fz_r.at[z], to_z(ZL * zz + l))

    for stages in ((gh_dot,), (gh_own, gh_core), (gh_relay,), (gh_z,)):
        for k in (2, 1, 3, 0):
            for stage in stages:
                stage(k)

    def gw_tile(i, _):
        lhs = jnp.concatenate([ht[r, i // 2, lax.rem(i, 2)].reshape(256, BATCH) for r in range(NX)], axis=1)
        gwv[i] = lax.dot_general(lhs, gall[...], (((1,), (1,)), ((), ())), preferred_element_type=F32).astype(BF)
        pltpu.make_async_copy(gwv.at[i], gw_hbm.at[i], gw_sem.at[i]).start()
        return 0

    lax.fori_loop(0, 8, gw_tile, 0)

    zrb[z] = rz[zs, zl0]

    def wait_fz(k, _):
        recv(zrb.at[zat(-k)], fz_r.at[zat(-k)])
        return 0

    lax.fori_loop(1, NZ, wait_fz, 0)
    gh_out[...] = jnp.sum(zrb[...].astype(F32), axis=0).astype(BF)

    def gw_wait(i, _):
        pltpu.make_async_copy(gwv.at[i], gw_hbm.at[i], gw_sem.at[i]).wait()
        return 0

    lax.fori_loop(0, 8, gw_wait, 0)

    for d in sends:
        d.wait_send()


def body(hidden, weight, labels, counts):
    dma = pltpu.SemaphoreType.DMA
    v = pltpu.VMEM
    scratch = [
        v((16, 2, 64, VL), BF),
        v((VL, 2048), BF),
        v((NZ, FEAT, BATCH), BF),
        v((NX, ZL, NC, NY, FEAT, BATCH), BF),
        v((NX, VL, BATCH), F32),
        v((256, BATCH), F32),
        v((256, BATCH), F32),
        v((VL, BATCH), F32),
        v((VL, BATCH), F32),
        v((NX, 1, VL), jnp.int32),
        v((NX, 1, BATCH), jnp.int32),
        v((VL, BATCH), F32),
        v((NX, VL, BATCH), BF),
        v((NZ, 8, BATCH), F32),
        v((8, 8, BATCH), F32),
        v((NX, 8, BATCH), F32),
        v((VL, NX * BATCH), BF),
        v((NX, ZL, NY, 16, 512), BF),
        v((NX, ZL, NY, 16, 512), F32),
        v((NX, ZL, NY, 16, 512), BF),
        v((NX, ZL, NY, 16, 512), BF),
        v((NX, 2, 16, 512), BF),
        v((NX, 2, 16, 512), BF),
        v((NX, 2, 16, 512), BF),
        v((NX, 2, 16, 512), BF),
        v((NX, ZL, 16, 512), BF),
        v((NX, ZL, 16, 512), BF),
        v((NX, ZL, 16, 512), BF),
        v((NZ, 16, 512), BF),
        v((8, 256, VL), BF),
        dma, dma((3,)), dma((8,)),
        dma((16,)), dma((16,)), dma((4,)), dma((4,)), dma((4,)), dma((4,)), dma((4,)), dma((4,)),
        dma((4, 4)), dma((4, 4)), dma((4,)), dma((4,)),
        dma((6,)), dma((6,)), dma((16,)), dma((16,)), dma((8,)), dma((8,)), dma((4,)), dma((4,)), dma((4,)), dma((4,)),
        dma((4,)), dma((4,)), dma((4, 6)), dma((4, 6)), dma((4, 4)), dma((16,)),
    ]
    vmem = pl.BlockSpec(memory_space=pltpu.VMEM)
    hbm = pl.BlockSpec(memory_space=pltpu.HBM)
    gw, gh, loss = pl.pallas_call(
        kernel,
        out_shape=(
            jax.ShapeDtypeStruct((8, 256, VL), BF),
            jax.ShapeDtypeStruct((16, 512), BF),
            jax.ShapeDtypeStruct((1,), F32),
        ),
        in_specs=[hbm] * 4,
        out_specs=(pl.BlockSpec(memory_space=pl.ANY), vmem, pl.BlockSpec(memory_space=pltpu.SMEM)),
        scratch_shapes=scratch,
        compiler_params=pltpu.CompilerParams(
            collective_id=0, has_side_effects=True, vmem_limit_bytes=63 * 1024 * 1024
        ),
        cost_estimate=pl.CostEstimate(flops=3 * 2**30, bytes_accessed=2**22, transcendentals=2**16),
    )(hidden.T, weight.reshape(16, 2, 64, VL), labels.reshape(1, BATCH), counts)
    return gw.reshape(2048, VL), gh, loss


def solution(mesh):
    in_specs = (
        P("dp", ("section", "tensor")),
        P("dp", ("section", "tensor")),
        P("dp"),
        P("dp", ("section", "tensor")),
    )
    out_specs = (P("dp", ("section", "tensor")), P(("dp", "section", "tensor"), None), P("dp"))
    return jax.shard_map(body, mesh=mesh, in_specs=in_specs, out_specs=out_specs, check_vma=False)
```

```python
import functools

import jax
import jax.numpy as jnp
from jax import lax
from jax.experimental import pallas as pl
from jax.experimental.pallas import tpu as pltpu
from jax.sharding import PartitionSpec as P

NX, NY, NZ, NC = 4, 4, 16, 2
ZL = NZ // NX
BATCH = 128
FEAT = 64
VL = 512
MESH = pl.DeviceIdType.MESH
BF = jnp.bfloat16
F32 = jnp.float32


GATHER = (
    ("yd", 0), ("yd", 2), ("yd", 1), ("yd", 3), ("cored", 2), ("cored", 1),
    ("logits", 2), ("cored", 3), ("logits", 1), ("cored", 0), ("logits", 3), ("logits", 0),
    ("sum", 3), ("sum", 1),
)
REDUCE = (
    ("dot", 2), ("dot", 1), ("dot", 3), ("dot", 0), ("own", 2), ("yd", 2), ("own", 1), ("y", 1), ("own", 3), ("y", 3),
    ("own", 0), ("y", 0), ("gw", 0), ("gw", 1), ("relay", 1), ("zd", 2), ("relay", 3), ("z", 1), ("relay", 0), ("gw", 2), ("z", 3),
    ("gw", 3), ("z", 0), ("gw", 4), ("gw", 5), ("gw", 6), ("gw", 7),
)


def spread(i):
    half = (i + 1) // 2
    return NZ // 2 + (1 - 2 * lax.rem(i, 2)) * half


def kernel(
    hid_hbm, w_hbm, lab_hbm, cnt_hbm,
    gw_hbm, gh_out, loss_out,
    wv, wt, zbuf, ht, part, bufa, bufb, rfl, rfr, cbuf, lbuf, fcol, eb, stz, sty, coef, gall,
    psend, pown, crecv, q, ya, yb, sa, sb, yl, yr, y2, rz, zrb, gwv,
    w_sem, in_sem, gw_sem,
    az_s, az_r, ax_s, ax_r, ct_s, ct_r, lb_s, lb_r, ay_s, ay_r, ac_s, ac_r,
    b_s, b_r, sz_s, sz_r, sy_s, sy_r, eb_s, eb_r, co_s, co_r,
    fc_s, fc_r, fy_s, fy_r, fz_s, fz_r,
):
    x = lax.axis_index("dp")
    s = lax.axis_index("section")
    y = lax.axis_index("tensor")
    z, c = s // 2, lax.rem(s, 2)
    zs, zl0 = z // ZL, lax.rem(z, ZL)
    oc = 1 - c

    def xat(k):
        return lax.rem(x + k + NX, NX)

    def yat(k):
        return lax.rem(y + k + NY, NY)

    def zat(k):
        return lax.rem(z + k + NZ, NZ)

    def to_x(k):
        return (xat(k), s, y)

    def to_y(k):
        return (x, s, yat(k))

    def to_z(zz):
        return (x, 2 * zz + c, y)

    def to_q(k):
        j = lax.rem(y * 2 + c + k, 8)
        return (x, 2 * z + lax.rem(j, 2), j // 2)

    sibling = (x, 2 * z + oc, y)
    sends = []

    def rcopy(src, dst, ss, rs, dev):
        return pltpu.make_async_remote_copy(
            src_ref=src, dst_ref=dst, send_sem=ss, recv_sem=rs, device_id=dev, device_id_type=MESH
        )

    def send(src, dst, ss, rs, dev):
        d = rcopy(src, dst, ss, rs, dev)
        d.start()
        sends.append(d)

    def recv(dst, rs):
        rcopy(dst, dst, rs, rs, sibling).wait_recv()

    w_copy = pltpu.make_async_copy(w_hbm, wv, w_sem)
    ins = [
        pltpu.make_async_copy(hid_hbm, zbuf.at[z], in_sem.at[0]),
        pltpu.make_async_copy(cnt_hbm, cbuf.at[x], in_sem.at[1]),
        pltpu.make_async_copy(lab_hbm, lbuf.at[x], in_sem.at[2]),
    ]
    for copy in ins:
        copy.start()

    barrier = pltpu.get_barrier_semaphore()

    def greet_z(i, _):
        pl.semaphore_signal(barrier, inc=1, device_id=to_z(zat(spread(i))), device_id_type=MESH)
        return 0

    lax.fori_loop(0, NZ - 1, greet_z, 0)
    for k in range(1, 8):
        pl.semaphore_signal(barrier, inc=1, device_id=to_q(k), device_id_type=MESH)
    for k in range(1, NX):
        pl.semaphore_signal(barrier, inc=1, device_id=to_x(k), device_id_type=MESH)
    w_copy.start()
    for copy in ins:
        copy.wait()
    pl.semaphore_wait(barrier, 25)

    def start_z(i, _):
        k = spread(i)
        rcopy(zbuf.at[z], zbuf.at[z], az_s.at[k], az_r.at[k], to_z(zat(k))).start()
        return 0

    lax.fori_loop(0, NZ - 1, start_z, 0)
    for k in range(1, NX):
        send(cbuf.at[x], cbuf.at[x], ct_s.at[k], ct_r.at[k], to_x(k))
        send(lbuf.at[x], lbuf.at[x], lb_s.at[k], lb_r.at[k], to_x(k))

    w_copy.wait()

    def turn(i, _):
        rows = wv[pl.ds(2 * i, 2)].reshape(256, VL)
        wt[:, pl.ds(pl.multiple_of(i * 256, 256), 256)] = rows.T
        return 0

    lax.fori_loop(0, 8, turn, 0)
    for k in range(1, NX):
        recv(cbuf.at[xat(-k)], ct_r.at[k])
        recv(lbuf.at[xat(-k)], lb_r.at[k])
    totals = cbuf[0] + cbuf[1] + cbuf[2] + cbuf[3]
    factor = lax.rsqrt(1.0 + totals.astype(F32))
    fcol[...] = jnp.broadcast_to(factor, (BATCH, VL)).T

    def wait_z(k, _):
        recv(zbuf.at[zat(-k)], az_r.at[k])
        rcopy(zbuf.at[z], zbuf.at[z], az_s.at[k], az_r.at[k], sibling).wait_send()
        return 0

    lax.fori_loop(1, NZ, wait_z, 0)

    for k in (2, 1, 3):
        to = xat(k)
        send(zbuf.at[pl.ds(ZL * to, ZL)], ht.at[x, :, c, y], ax_s.at[k], ax_r.at[k], to_x(k))
    ht[x, :, c, y] = zbuf[pl.ds(ZL * x, ZL)]

    def hid_y(k):
        r = xat(-k)
        if k:
            recv(ht.at[r, :, c, y], ax_r.at[k])
        for d, e in ((0, 1), (1, -1)):
            send(ht.at[r, :, c, y], ht.at[r, :, c, y], ay_s.at[k, d], ay_r.at[k, d], to_y(e))

    def hid_yd(k):
        r = xat(-k)
        if k:
            recv(ht.at[r, :, c, y], ax_r.at[k])
        for d, e in ((2, 2), (0, 1), (1, -1)):
            send(ht.at[r, :, c, y], ht.at[r, :, c, y], ay_s.at[k, d], ay_r.at[k, d], to_y(e))

    def hid_cored(k):
        r = xat(-k)
        for d, e in ((0, 1), (1, -1), (2, 2)):
            recv(ht.at[r, :, c, yat(-e)], ay_r.at[k, d])
        send(ht.at[r, :, c], ht.at[r, :, c], ac_s.at[k], ac_r.at[k], sibling)

    def hid_relay(k):
        r = xat(-k)
        for d, e in ((0, 1), (1, -1)):
            recv(ht.at[r, :, c, yat(-e)], ay_r.at[k, d])
            half = pl.ds(2 * d, 2)
            ref = ht.at[r, half, c, yat(-e)]
            send(ref, ref, ay_s.at[k, 2 + d], ay_r.at[k, 2 + d], to_y(e))

    def hid_core(k):
        r = xat(-k)
        for d in (0, 1):
            recv(ht.at[r, pl.ds(2 * d, 2), c, yat(2)], ay_r.at[k, 2 + d])
        send(ht.at[r, :, c], ht.at[r, :, c], ac_s.at[k], ac_r.at[k], sibling)

    def logits_of(k):
        r = xat(-k)
        recv(ht.at[r, :, oc], ac_r.at[k])

        def tile(i, _):
            rows = pl.ds(pl.multiple_of(i * 256, 256), 256)
            part[r, rows] = jnp.dot(wt[rows, :], ht[r].reshape(2048, BATCH), preferred_element_type=F32)
            return 0

        lax.fori_loop(0, 2, tile, 0)
        top, low = pl.ds(0, 256), pl.ds(256, 256)
        if k == 2:
            send(part.at[r, top], bufa, b_s.at[0], b_r.at[0], to_x(1))
            send(part.at[r, low], bufb, b_s.at[1], b_r.at[1], to_x(-1))
        if k == 3:
            send(part.at[r, low], rfl.at[low], b_s.at[2], b_r.at[2], to_x(1))
        if k == 1:
            send(part.at[r, top], rfr.at[top], b_s.at[4], b_r.at[4], to_x(-1))

    def logits_relay(k):
        r = xat(-k)
        top, low = pl.ds(0, 256), pl.ds(256, 256)
        if k == 3:
            recv(bufa, b_r.at[0])
            part[r, top] = part[r, top] + bufa[...]
            send(part.at[r, top], rfl.at[top], b_s.at[3], b_r.at[3], to_x(1))
        if k == 1:
            recv(bufb, b_r.at[1])
            part[r, low] = part[r, low] + bufb[...]
            send(part.at[r, low], rfr.at[low], b_s.at[5], b_r.at[5], to_x(-1))

    run = {
        "y": hid_y, "yd": hid_yd, "relay": hid_relay, "core": hid_core, "cored": hid_cored,
        "logits": logits_of, "sum": logits_relay,
    }
    for name, k in GATHER:
        run[name](k)

    top, low = pl.ds(0, 256), pl.ds(256, 256)
    recv(rfl.at[low], b_r.at[2])
    recv(rfl.at[top], b_r.at[3])
    recv(rfr.at[top], b_r.at[4])
    recv(rfr.at[low], b_r.at[5])

    logits = part[x] + rfl[...] + rfr[...]
    ids = lax.broadcasted_iota(jnp.int32, (VL, BATCH), 0) + (s * NY + y) * VL
    hit = ids == lbuf[x]
    m0 = jnp.max(logits, axis=0, keepdims=True)
    e0 = jnp.exp(logits - m0)
    eb[x] = e0.astype(BF)
    for k in (2, 1, 3):
        send(eb.at[x], eb.at[x], eb_s.at[k], eb_r.at[k], to_x(k))
    zero = jnp.zeros((4, BATCH), F32)
    stz[z] = jnp.concatenate(
        [
            m0,
            jnp.sum(e0, axis=0, keepdims=True),
            jnp.sum(jnp.where(hit, logits, 0.0), axis=0, keepdims=True),
            jnp.sum(jnp.where(hit, fcol[...], 0.0), axis=0, keepdims=True),
            zero,
        ],
        axis=0,
    )

    def combine(ref):
        v = ref[...]
        tops = v[:, 0:1, :]
        m = jnp.max(tops, axis=0)
        t = jnp.sum(v[:, 1:2, :] * jnp.exp(tops - m[None]), axis=0)
        return m, t, jnp.sum(v[:, 2:3, :], axis=0), jnp.sum(v[:, 3:4, :], axis=0)

    def start_sz(i, _):
        k = spread(i)
        rcopy(stz.at[z], stz.at[z], sz_s.at[k], sz_r.at[k], to_z(zat(k))).start()
        return 0

    def wait_sz(k, _):
        recv(stz.at[zat(-k)], sz_r.at[k])
        rcopy(stz.at[z], stz.at[z], sz_s.at[k], sz_r.at[k], sibling).wait_send()
        return 0

    lax.fori_loop(0, NZ - 1, start_sz, 0)
    lax.fori_loop(1, NZ, wait_sz, 0)
    me = y * 2 + c
    sty[me] = jnp.concatenate([*combine(stz), zero], axis=0)
    for k in range(1, 8):
        send(sty.at[me], sty.at[me], sy_s.at[k], sy_r.at[k], to_q(k))
    for k in range(1, 8):
        recv(sty.at[lax.rem(me - k + 8, 8)], sy_r.at[k])
    m, total, target, weight = combine(sty)
    scaled = weight / jnp.mean(weight)
    loss_out[0] = jnp.sum(scaled * (jnp.log(total) + m - target)) / BATCH
    coef[x] = jnp.concatenate([scaled * jnp.exp(m0 - m) / total, scaled, jnp.zeros((6, BATCH), F32)], axis=0)

    for k in (2, 1, 3):
        send(coef.at[x], coef.at[x], co_s.at[k], co_r.at[k], to_x(k))
    for k in (0, 1, 3, 2):
        r = xat(-k)
        if k:
            recv(eb.at[r], eb_r.at[k])
            recv(coef.at[r], co_r.at[k])
        v = coef[r]
        gall[:, pl.ds(pl.multiple_of(r * BATCH, BATCH), BATCH)] = (
            eb[r].astype(F32) * v[0:1] - jnp.where(ids == lbuf[r], v[1:2], 0.0)
        ).astype(BF)
    def gh_dot(k):
        zz = lax.rem(zs + k, NX)
        rows = wv[pl.ds(ZL * zz, ZL), oc].reshape(256, VL)
        psend[zz] = jnp.dot(rows, gall[...], preferred_element_type=F32).astype(BF).reshape(ZL, NY, 16, 512)
        send(psend.at[zz], crecv.at[zz], fc_s.at[k], fc_r.at[k], sibling)

    def gh_own(k):
        zz = lax.rem(zs + k, NX)
        rows = wv[pl.ds(ZL * zz, ZL), c].reshape(256, VL)
        pown[zz] = jnp.dot(rows, gall[...], preferred_element_type=F32).reshape(ZL, NY, 16, 512)
        recv(crecv.at[zz], fc_r.at[k])
        q[zz] = (pown[zz] + crecv[zz].astype(F32)).astype(BF)

    def gh_yd(k):
        zz = lax.rem(zs + k, NX)
        send(q.at[zz, :, yat(2)], y2.at[k], fy_s.at[k, 2], fy_r.at[k, 2], to_y(2))
        send(q.at[zz, :, yat(1)], yl.at[k], fy_s.at[k, 0], fy_r.at[k, 0], to_y(1))
        send(q.at[zz, :, yat(-1)], yr.at[k], fy_s.at[k, 1], fy_r.at[k, 1], to_y(-1))

    def gh_y(k):
        zz = lax.rem(zs + k, NX)
        up, down = pl.ds(0, 2), pl.ds(2, 2)
        send(q.at[zz, up, yat(2)], ya.at[k], fy_s.at[k, 0], fy_r.at[k, 0], to_y(1))
        send(q.at[zz, down, yat(2)], yb.at[k], fy_s.at[k, 1], fy_r.at[k, 1], to_y(-1))
        send(q.at[zz, down, yat(1)], yl.at[k, down], fy_s.at[k, 2], fy_r.at[k, 2], to_y(1))
        send(q.at[zz, up, yat(-1)], yr.at[k, up], fy_s.at[k, 3], fy_r.at[k, 3], to_y(-1))

    def gh_relay(k):
        zz = lax.rem(zs + k, NX)
        up, down = pl.ds(0, 2), pl.ds(2, 2)
        recv(ya.at[k], fy_r.at[k, 0])
        sa[k] = (q[zz, up, yat(1)].astype(F32) + ya[k].astype(F32)).astype(BF)
        send(sa.at[k], yl.at[k, up], fy_s.at[k, 4], fy_r.at[k, 4], to_y(1))
        recv(yb.at[k], fy_r.at[k, 1])
        sb[k] = (q[zz, down, yat(-1)].astype(F32) + yb[k].astype(F32)).astype(BF)
        send(sb.at[k], yr.at[k, down], fy_s.at[k, 5], fy_r.at[k, 5], to_y(-1))

    def gh_z(k):
        zz = lax.rem(zs + k, NX)
        up, down = pl.ds(0, 2), pl.ds(2, 2)
        recv(yl.at[k, down], fy_r.at[k, 2])
        recv(yr.at[k, up], fy_r.at[k, 3])
        recv(yl.at[k, up], fy_r.at[k, 4])
        recv(yr.at[k, down], fy_r.at[k, 5])
        rz[zz] = (q[zz, :, y].astype(F32) + yl[k].astype(F32) + yr[k].astype(F32)).astype(BF)
        gh_send(k)

    def gh_zd(k):
        zz = lax.rem(zs + k, NX)
        for ref, d in ((yl, 0), (yr, 1), (y2, 2)):
            recv(ref.at[k], fy_r.at[k, d])
        near = yl[k].astype(F32) + yr[k].astype(F32)
        rz[zz] = (q[zz, :, y].astype(F32) + near + y2[k].astype(F32)).astype(BF)
        gh_send(k)

    def gh_send(k):
        zz = lax.rem(zs + k, NX)
        for j in range(0 if k else 1, ZL):
            l = lax.rem(zl0 + j, ZL)
            send(rz.at[zz, l], zrb.at[z], fz_s.at[k, j], fz_r.at[z], to_z(ZL * zz + l))

    def gw_tile(i):
        lhs = jnp.concatenate([ht[r, i // 2, i % 2].reshape(256, BATCH) for r in range(NX)], axis=1)
        gwv[i] = lax.dot_general(lhs, gall[...], (((1,), (1,)), ((), ())), preferred_element_type=F32).astype(BF)
        pltpu.make_async_copy(gwv.at[i], gw_hbm.at[i], gw_sem.at[i]).start()

    run = {
        "dot": gh_dot, "own": gh_own, "y": gh_y, "yd": gh_yd, "relay": gh_relay, "z": gh_z, "zd": gh_zd, "gw": gw_tile,
    }
    for name, k in REDUCE:
        run[name](k)

    zrb[z] = rz[zs, zl0]

    def wait_fz(k, _):
        recv(zrb.at[zat(-k)], fz_r.at[zat(-k)])
        return 0

    lax.fori_loop(1, NZ, wait_fz, 0)
    gh_out[...] = jnp.sum(zrb[...].astype(F32), axis=0).astype(BF)

    def gw_wait(i, _):
        pltpu.make_async_copy(gwv.at[i], gw_hbm.at[i], gw_sem.at[i]).wait()
        return 0

    lax.fori_loop(0, 8, gw_wait, 0)

    for d in sends:
        d.wait_send()


def hand_over(*refs):
    ins, outs, bufs, (in_sem, out_sem) = refs[:3], refs[3:6], refs[6:9], refs[9:]
    pieces = [(0, i) for i in range(8)] + [(1, None), (2, None)]

    def copy(src, dst, piece, sem):
        j, i = piece
        n = pieces.index(piece)
        a, b = (src[j], dst[j]) if i is None else (src[j].at[i], dst[j].at[i])
        return pltpu.make_async_copy(a, b, sem.at[n])

    for piece in pieces:
        copy(ins, bufs, piece, in_sem).start()
    for piece in pieces:
        copy(ins, bufs, piece, in_sem).wait()
        copy(bufs, outs, piece, out_sem).start()
    for piece in pieces:
        copy(bufs, outs, piece, out_sem).wait()


def body(hidden, weight, labels, counts):
    dma = pltpu.SemaphoreType.DMA
    v = pltpu.VMEM
    scratch = [
        v((16, 2, 64, VL), BF),
        v((VL, 2048), BF),
        v((NZ, FEAT, BATCH), BF),
        v((NX, ZL, NC, NY, FEAT, BATCH), BF),
        v((NX, VL, BATCH), F32),
        v((256, BATCH), F32),
        v((256, BATCH), F32),
        v((VL, BATCH), F32),
        v((VL, BATCH), F32),
        v((NX, 1, VL), jnp.int32),
        v((NX, 1, BATCH), jnp.int32),
        v((VL, BATCH), F32),
        v((NX, VL, BATCH), BF),
        v((NZ, 8, BATCH), F32),
        v((8, 8, BATCH), F32),
        v((NX, 8, BATCH), F32),
        v((VL, NX * BATCH), BF),
        v((NX, ZL, NY, 16, 512), BF),
        v((NX, ZL, NY, 16, 512), F32),
        v((NX, ZL, NY, 16, 512), BF),
        v((NX, ZL, NY, 16, 512), BF),
        v((NX, 2, 16, 512), BF),
        v((NX, 2, 16, 512), BF),
        v((NX, 2, 16, 512), BF),
        v((NX, 2, 16, 512), BF),
        v((NX, ZL, 16, 512), BF),
        v((NX, ZL, 16, 512), BF),
        v((NX, ZL, 16, 512), BF),
        v((NX, ZL, 16, 512), BF),
        v((NZ, 16, 512), BF),
        v((8, 256, VL), BF),
        dma, dma((3,)), dma((8,)),
        dma((16,)), dma((16,)), dma((4,)), dma((4,)), dma((4,)), dma((4,)), dma((4,)), dma((4,)),
        dma((4, 4)), dma((4, 4)), dma((4,)), dma((4,)),
        dma((6,)), dma((6,)), dma((16,)), dma((16,)), dma((8,)), dma((8,)), dma((4,)), dma((4,)), dma((4,)), dma((4,)),
        dma((4,)), dma((4,)), dma((4, 6)), dma((4, 6)), dma((4, 4)), dma((16,)),
    ]
    vmem = pl.BlockSpec(memory_space=pltpu.VMEM)
    hbm = pl.BlockSpec(memory_space=pltpu.HBM)
    shapes = (
        jax.ShapeDtypeStruct((8, 256, VL), BF),
        jax.ShapeDtypeStruct((16, 512), BF),
        jax.ShapeDtypeStruct((1,), F32),
    )
    smem = pl.BlockSpec(memory_space=pltpu.SMEM)
    made = pl.pallas_call(
        kernel,
        out_shape=shapes,
        in_specs=[hbm] * 4,
        out_specs=(pl.BlockSpec(memory_space=pl.ANY), vmem, smem),
        scratch_shapes=scratch,
        compiler_params=pltpu.CompilerParams(
            collective_id=0, has_side_effects=True, vmem_limit_bytes=63 * 1024 * 1024
        ),
        cost_estimate=pl.CostEstimate(flops=3 * 2**30, bytes_accessed=2**22, transcendentals=2**16),
    )(hidden.T, weight.reshape(16, 2, 64, VL), labels.reshape(1, BATCH), counts)
    gw, gh, loss = pl.pallas_call(
        hand_over,
        out_shape=shapes,
        in_specs=[hbm] * 3,
        out_specs=(hbm,) * 3,
        scratch_shapes=[
            v((8, 256, VL), BF), v((16, 512), BF), pltpu.SMEM((1,), F32), dma((10,)), dma((10,)),
        ],
    )(*made)
    return gw.reshape(2048, VL), gh, loss


def solution(mesh):
    in_specs = (
        P("dp", ("section", "tensor")),
        P("dp", ("section", "tensor")),
        P("dp"),
        P("dp", ("section", "tensor")),
    )
    out_specs = (P("dp", ("section", "tensor")), P(("dp", "section", "tensor"), None), P("dp"))
    return jax.shard_map(body, mesh=mesh, in_specs=in_specs, out_specs=out_specs, check_vma=False)
```

```python
import functools

import jax
import jax.numpy as jnp
from jax import lax
from jax.experimental import pallas as pl
from jax.experimental.pallas import tpu as pltpu
from jax.sharding import PartitionSpec as P

NX, NY, NZ, NC = 4, 4, 16, 2
ZL = NZ // NX
BATCH = 128
FEAT = 64
VL = 512
MESH = pl.DeviceIdType.MESH
BF = jnp.bfloat16
F32 = jnp.float32


GATHER = (
    ("x", 0, 0),
    ("y", 2, 0), ("y", 1, 0), ("y", 3, 0),  ("x", 0, 1), ("y", 2, 1), ("y", 1, 1), ("y", 3, 1),
    ("core", 2), ("core", 1), ("logits", 2), ("core", 3), ("logits", 1), ("core", 0), ("logits", 3), ("logits", 0),
    ("sum", 3), ("sum", 1),
)
REDUCE = (
    ("dot", 2), ("dot", 1), ("dot", 3), ("dot", 0), ("own", 2), ("yd", 2, 0), ("yd", 2, 1), ("own", 1), ("yd", 1, 0), ("yd", 1, 1),
    ("own", 3), ("yd", 3, 0), ("yd", 3, 1), ("own", 0), ("y", 0), ("gw", 0), ("gw", 1), ("zd", 2, 0), ("zd", 2, 1), ("relay", 0),
    ("zd", 1, 0), ("zd", 1, 1), ("zd", 3, 0), ("zd", 3, 1), ("gw", 2), ("gw", 3), ("z", 0), ("gw", 4), ("gw", 5), ("gw", 6), ("gw", 7),
)


def spread(i):
    half = (i + 1) // 2
    return NZ // 2 + (1 - 2 * lax.rem(i, 2)) * half


def kernel(
    hid_hbm, w_hbm, lab_hbm, cnt_hbm,
    gwv, gh_out, loss_out,
    wv, wt, zbuf, ht, part, bufa, bufb, rfl, rfr, cbuf, lbuf, fcol, eb, stz, sty, coef, gall,
    psend, pown, crecv, q, ya, yb, sa, sb, yl, yr, y2, rz, zrb,
    w_sem, in_sem,
    az_s, az_r, ax_s, ax_r, ct_s, ct_r, lb_s, lb_r, ay_s, ay_r, ac_s, ac_r,
    b_s, b_r, sz_s, sz_r, sy_s, sy_r, eb_s, eb_r, co_s, co_r,
    fc_s, fc_r, fy_s, fy_r, fz_s, fz_r,
):
    x = lax.axis_index("dp")
    s = lax.axis_index("section")
    y = lax.axis_index("tensor")
    z, c = s // 2, lax.rem(s, 2)
    zs, zl0 = z // ZL, lax.rem(z, ZL)
    oc = 1 - c

    def xat(k):
        return lax.rem(x + k + NX, NX)

    def yat(k):
        return lax.rem(y + k + NY, NY)

    def zat(k):
        return lax.rem(z + k + NZ, NZ)

    def to_x(k):
        return (xat(k), s, y)

    def to_y(k):
        return (x, s, yat(k))

    def to_z(zz):
        return (x, 2 * zz + c, y)

    def to_q(k):
        j = lax.rem(y * 2 + c + k, 8)
        return (x, 2 * z + lax.rem(j, 2), j // 2)

    sibling = (x, 2 * z + oc, y)
    sends = []

    def rcopy(src, dst, ss, rs, dev):
        return pltpu.make_async_remote_copy(
            src_ref=src, dst_ref=dst, send_sem=ss, recv_sem=rs, device_id=dev, device_id_type=MESH
        )

    def send(src, dst, ss, rs, dev):
        d = rcopy(src, dst, ss, rs, dev)
        d.start()
        sends.append(d)

    def play(run, schedule):
        for name, *at in schedule:
            run[name](*at)

    def recv(dst, rs):
        rcopy(dst, dst, rs, rs, sibling).wait_recv()

    w_copy = pltpu.make_async_copy(w_hbm, wv, w_sem)
    ins = [
        pltpu.make_async_copy(hid_hbm, zbuf.at[z], in_sem.at[0]),
        pltpu.make_async_copy(cnt_hbm, cbuf.at[x], in_sem.at[1]),
        pltpu.make_async_copy(lab_hbm, lbuf.at[x], in_sem.at[2]),
    ]
    for copy in ins:
        copy.start()

    barrier = pltpu.get_barrier_semaphore()

    def greet_z(i, _):
        pl.semaphore_signal(barrier, inc=1, device_id=to_z(zat(spread(i))), device_id_type=MESH)
        return 0

    lax.fori_loop(0, NZ - 1, greet_z, 0)
    for k in range(1, 8):
        pl.semaphore_signal(barrier, inc=1, device_id=to_q(k), device_id_type=MESH)
    for k in range(1, NX):
        pl.semaphore_signal(barrier, inc=1, device_id=to_x(k), device_id_type=MESH)
    w_copy.start()
    for copy in ins:
        copy.wait()
    pl.semaphore_wait(barrier, 25)

    halves = [pl.ds(0, FEAT // 2), pl.ds(FEAT // 2, FEAT // 2)]

    def start_z(h):
        def start(i, _):
            k = spread(i)
            ref = zbuf.at[z, halves[h]]
            rcopy(ref, ref, az_s.at[h, k], az_r.at[h, k], to_z(zat(k))).start()
            return 0

        lax.fori_loop(0, NZ - 1, start, 0)

    start_z(0)
    start_z(1)
    for k in range(1, NX):
        send(cbuf.at[x], cbuf.at[x], ct_s.at[k], ct_r.at[k], to_x(k))
        send(lbuf.at[x], lbuf.at[x], lb_s.at[k], lb_r.at[k], to_x(k))

    w_copy.wait()

    def turn(i, _):
        rows = wv[pl.ds(2 * i, 2)].reshape(256, VL)
        wt[:, pl.ds(pl.multiple_of(i * 256, 256), 256)] = rows.T
        return 0

    lax.fori_loop(0, 8, turn, 0)
    for k in range(1, NX):
        recv(cbuf.at[xat(-k)], ct_r.at[k])
        recv(lbuf.at[xat(-k)], lb_r.at[k])
    totals = cbuf[0] + cbuf[1] + cbuf[2] + cbuf[3]
    factor = lax.rsqrt(1.0 + totals.astype(F32))
    fcol[...] = jnp.broadcast_to(factor, (BATCH, VL)).T

    def hid_x(_, h):
        def wait_z(k, _):
            ref = zbuf.at[z, halves[h]]
            recv(zbuf.at[zat(-k), halves[h]], az_r.at[h, k])
            rcopy(ref, ref, az_s.at[h, k], az_r.at[h, k], sibling).wait_send()
            return 0

        lax.fori_loop(1, NZ, wait_z, 0)
        for k in (2, 1, 3):
            to = xat(k)
            send(
                zbuf.at[pl.ds(ZL * to, ZL), halves[h]], ht.at[x, :, c, y, halves[h]],
                ax_s.at[h, k], ax_r.at[h, k], to_x(k),
            )
        ht[x, :, c, y, halves[h]] = zbuf[pl.ds(ZL * x, ZL), halves[h]]
        hid_y(0, h)

    def hid_y(k, h):
        r = xat(-k)
        ref = ht.at[r, :, c, y, halves[h]]
        if k:
            recv(ref, ax_r.at[h, k])
        for e in (2, 1, 3):
            send(ref, ref, ay_s.at[h, k, e], ay_r.at[h, k, e], to_y(e))

    def hid_core(k):
        r = xat(-k)
        for h in (0, 1):
            for e in (1, 3, 2):
                recv(ht.at[r, :, c, yat(-e), halves[h]], ay_r.at[h, k, e])
        send(ht.at[r, :, c], ht.at[r, :, c], ac_s.at[k], ac_r.at[k], sibling)

    def logits_of(k):
        r = xat(-k)
        recv(ht.at[r, :, oc], ac_r.at[k])

        def tile(i, _):
            rows = pl.ds(pl.multiple_of(i * 256, 256), 256)
            part[r, rows] = jnp.dot(wt[rows, :], ht[r].reshape(2048, BATCH), preferred_element_type=F32)
            return 0

        lax.fori_loop(0, 2, tile, 0)
        top, low = pl.ds(0, 256), pl.ds(256, 256)
        if k == 2:
            send(part.at[r, top], bufa, b_s.at[0], b_r.at[0], to_x(1))
            send(part.at[r, low], bufb, b_s.at[1], b_r.at[1], to_x(-1))
        if k == 3:
            send(part.at[r, low], rfl.at[low], b_s.at[2], b_r.at[2], to_x(1))
        if k == 1:
            send(part.at[r, top], rfr.at[top], b_s.at[4], b_r.at[4], to_x(-1))

    def logits_relay(k):
        r = xat(-k)
        top, low = pl.ds(0, 256), pl.ds(256, 256)
        if k == 3:
            recv(bufa, b_r.at[0])
            part[r, top] = part[r, top] + bufa[...]
            send(part.at[r, top], rfl.at[top], b_s.at[3], b_r.at[3], to_x(1))
        if k == 1:
            recv(bufb, b_r.at[1])
            part[r, low] = part[r, low] + bufb[...]
            send(part.at[r, low], rfr.at[low], b_s.at[5], b_r.at[5], to_x(-1))

    run = {"x": hid_x, "y": hid_y, "core": hid_core, "logits": logits_of, "sum": logits_relay}
    play(run, GATHER)

    top, low = pl.ds(0, 256), pl.ds(256, 256)
    recv(rfl.at[low], b_r.at[2])
    recv(rfl.at[top], b_r.at[3])
    recv(rfr.at[top], b_r.at[4])
    recv(rfr.at[low], b_r.at[5])

    logits = part[x] + rfl[...] + rfr[...]
    ids = lax.broadcasted_iota(jnp.int32, (VL, BATCH), 0) + (s * NY + y) * VL
    hit = ids == lbuf[x]
    m0 = jnp.max(logits, axis=0, keepdims=True)
    e0 = jnp.exp(logits - m0)
    eb[x] = e0.astype(BF)
    for k in (2, 1, 3):
        send(eb.at[x], eb.at[x], eb_s.at[k], eb_r.at[k], to_x(k))
    zero = jnp.zeros((4, BATCH), F32)
    stz[z] = jnp.concatenate(
        [
            m0,
            jnp.sum(e0, axis=0, keepdims=True),
            jnp.sum(jnp.where(hit, logits, 0.0), axis=0, keepdims=True),
            jnp.sum(jnp.where(hit, fcol[...], 0.0), axis=0, keepdims=True),
            zero,
        ],
        axis=0,
    )

    def combine(ref):
        v = ref[...]
        tops = v[:, 0:1, :]
        m = jnp.max(tops, axis=0)
        t = jnp.sum(v[:, 1:2, :] * jnp.exp(tops - m[None]), axis=0)
        return m, t, jnp.sum(v[:, 2:3, :], axis=0), jnp.sum(v[:, 3:4, :], axis=0)

    def start_sz(i, _):
        k = spread(i)
        rcopy(stz.at[z], stz.at[z], sz_s.at[k], sz_r.at[k], to_z(zat(k))).start()
        return 0

    def wait_sz(k, _):
        recv(stz.at[zat(-k)], sz_r.at[k])
        rcopy(stz.at[z], stz.at[z], sz_s.at[k], sz_r.at[k], sibling).wait_send()
        return 0

    lax.fori_loop(0, NZ - 1, start_sz, 0)
    lax.fori_loop(1, NZ, wait_sz, 0)
    me = y * 2 + c
    sty[me] = jnp.concatenate([*combine(stz), zero], axis=0)
    for k in range(1, 8):
        send(sty.at[me], sty.at[me], sy_s.at[k], sy_r.at[k], to_q(k))
    for k in range(1, 8):
        recv(sty.at[lax.rem(me - k + 8, 8)], sy_r.at[k])
    m, total, target, weight = combine(sty)
    scaled = weight / jnp.mean(weight)
    loss_out[0] = jnp.sum(scaled * (jnp.log(total) + m - target)) / BATCH
    coef[x] = jnp.concatenate([scaled * jnp.exp(m0 - m) / total, scaled, jnp.zeros((6, BATCH), F32)], axis=0)

    for k in (2, 1, 3):
        send(coef.at[x], coef.at[x], co_s.at[k], co_r.at[k], to_x(k))
    for k in (0, 1, 3, 2):
        r = xat(-k)
        if k:
            recv(eb.at[r], eb_r.at[k])
            recv(coef.at[r], co_r.at[k])
        v = coef[r]
        gall[:, pl.ds(pl.multiple_of(r * BATCH, BATCH), BATCH)] = (
            eb[r].astype(F32) * v[0:1] - jnp.where(ids == lbuf[r], v[1:2], 0.0)
        ).astype(BF)
    def gh_dot(k):
        zz = lax.rem(zs + k, NX)
        rows = wv[pl.ds(ZL * zz, ZL), oc].reshape(256, VL)
        psend[zz] = jnp.dot(rows, gall[...], preferred_element_type=F32).astype(BF).reshape(ZL, NY, 16, 512)
        send(psend.at[zz], crecv.at[zz], fc_s.at[k], fc_r.at[k], sibling)

    def gh_own(k):
        zz = lax.rem(zs + k, NX)
        rows = wv[pl.ds(ZL * zz, ZL), c].reshape(256, VL)
        pown[zz] = jnp.dot(rows, gall[...], preferred_element_type=F32).reshape(ZL, NY, 16, 512)
        recv(crecv.at[zz], fc_r.at[k])
        q[zz] = (pown[zz] + crecv[zz].astype(F32)).astype(BF)

    def gh_yd(k, h):
        zz = lax.rem(zs + k, NX)
        two = pl.ds(2 * h, 2)
        for e, ref in ((2, y2), (1, yl), (3, yr)):
            n = 3 * h + e - 1
            send(q.at[zz, two, yat(e)], ref.at[k, two], fy_s.at[k, n], fy_r.at[k, n], to_y(e))

    def gh_y(k):
        zz = lax.rem(zs + k, NX)
        up, down = pl.ds(0, 2), pl.ds(2, 2)
        send(q.at[zz, up, yat(2)], ya.at[k], fy_s.at[k, 0], fy_r.at[k, 0], to_y(1))
        send(q.at[zz, down, yat(2)], yb.at[k], fy_s.at[k, 1], fy_r.at[k, 1], to_y(-1))
        send(q.at[zz, down, yat(1)], yl.at[k, down], fy_s.at[k, 2], fy_r.at[k, 2], to_y(1))
        send(q.at[zz, up, yat(-1)], yr.at[k, up], fy_s.at[k, 3], fy_r.at[k, 3], to_y(-1))

    def gh_relay(k):
        zz = lax.rem(zs + k, NX)
        up, down = pl.ds(0, 2), pl.ds(2, 2)
        recv(ya.at[k], fy_r.at[k, 0])
        sa[k] = (q[zz, up, yat(1)].astype(F32) + ya[k].astype(F32)).astype(BF)
        send(sa.at[k], yl.at[k, up], fy_s.at[k, 4], fy_r.at[k, 4], to_y(1))
        recv(yb.at[k], fy_r.at[k, 1])
        sb[k] = (q[zz, down, yat(-1)].astype(F32) + yb[k].astype(F32)).astype(BF)
        send(sb.at[k], yr.at[k, down], fy_s.at[k, 5], fy_r.at[k, 5], to_y(-1))

    def gh_z(k):
        zz = lax.rem(zs + k, NX)
        up, down = pl.ds(0, 2), pl.ds(2, 2)
        recv(yl.at[k, down], fy_r.at[k, 2])
        recv(yr.at[k, up], fy_r.at[k, 3])
        recv(yl.at[k, up], fy_r.at[k, 4])
        recv(yr.at[k, down], fy_r.at[k, 5])
        rz[zz] = (q[zz, :, y].astype(F32) + yl[k].astype(F32) + yr[k].astype(F32)).astype(BF)
        for j in range(0 if k else 1, ZL):
            l = lax.rem(zl0 + j, ZL)
            send(rz.at[zz, l], zrb.at[z], fz_s.at[k, j], fz_r.at[z], to_z(ZL * zz + l))

    def gh_zd(k, h):
        zz = lax.rem(zs + k, NX)
        two = pl.ds(2 * h, 2)
        for e, ref in ((1, yl), (3, yr), (2, y2)):
            recv(ref.at[k, two], fy_r.at[k, 3 * h + e - 1])
        near = yl[k, two].astype(F32) + yr[k, two].astype(F32)
        rz[zz, two] = (q[zz, two, y].astype(F32) + near + y2[k, two].astype(F32)).astype(BF)
        for j in (2 * h, 2 * h + 1):
            send(rz.at[zz, j], zrb.at[z], fz_s.at[k, j], fz_r.at[z], to_z(ZL * zz + j))

    def gw_tile(i):
        lhs = jnp.concatenate([ht[r, i // 2, i % 2].reshape(256, BATCH) for r in range(NX)], axis=1)
        gwv[i] = lax.dot_general(lhs, gall[...], (((1,), (1,)), ((), ())), preferred_element_type=F32).astype(BF)

    run = {
        "dot": gh_dot, "own": gh_own, "y": gh_y, "yd": gh_yd, "relay": gh_relay, "z": gh_z, "zd": gh_zd, "gw": gw_tile,
    }
    play(run, REDUCE)

    zrb[z] = rz[zs, zl0]

    def wait_fz(k, _):
        recv(zrb.at[zat(-k)], fz_r.at[zat(-k)])
        return 0

    lax.fori_loop(1, NZ, wait_fz, 0)
    gh_out[...] = jnp.sum(zrb[...].astype(F32), axis=0).astype(BF)

    for d in sends:
        d.wait_send()


def hand_over(gw_in, gh_in, loss_in, gw_out, gh_out, loss_out, held, sem):
    copies = [pltpu.make_async_copy(gw_in.at[i], gw_out.at[i], sem.at[i]) for i in range(8)]
    copies.append(pltpu.make_async_copy(gh_in, gh_out, sem.at[8]))
    first = pltpu.make_async_copy(loss_in, held, sem.at[9])
    first.start()
    for copy in copies:
        copy.start()
    first.wait()
    copies.append(pltpu.make_async_copy(held, loss_out, sem.at[9]))
    copies[-1].start()
    for copy in copies:
        copy.wait()


def body(hidden, weight, labels, counts):
    dma = pltpu.SemaphoreType.DMA
    v = pltpu.VMEM
    scratch = [
        v((16, 2, 64, VL), BF),
        v((VL, 2048), BF),
        v((NZ, FEAT, BATCH), BF),
        v((NX, ZL, NC, NY, FEAT, BATCH), BF),
        v((NX, VL, BATCH), F32),
        v((256, BATCH), F32),
        v((256, BATCH), F32),
        v((VL, BATCH), F32),
        v((VL, BATCH), F32),
        v((NX, 1, VL), jnp.int32),
        v((NX, 1, BATCH), jnp.int32),
        v((VL, BATCH), F32),
        v((NX, VL, BATCH), BF),
        v((NZ, 8, BATCH), F32),
        v((8, 8, BATCH), F32),
        v((NX, 8, BATCH), F32),
        v((VL, NX * BATCH), BF),
        v((NX, ZL, NY, 16, 512), BF),
        v((NX, ZL, NY, 16, 512), F32),
        v((NX, ZL, NY, 16, 512), BF),
        v((NX, ZL, NY, 16, 512), BF),
        v((NX, 2, 16, 512), BF),
        v((NX, 2, 16, 512), BF),
        v((NX, 2, 16, 512), BF),
        v((NX, 2, 16, 512), BF),
        v((NX, ZL, 16, 512), BF),
        v((NX, ZL, 16, 512), BF),
        v((NX, ZL, 16, 512), BF),
        v((NX, ZL, 16, 512), BF),
        v((NZ, 16, 512), BF),
        dma, dma((3,)),
        dma((2, 16)), dma((2, 16)), dma((2, 4)), dma((2, 4)), dma((4,)), dma((4,)), dma((4,)), dma((4,)),
        dma((2, 4, 4)), dma((2, 4, 4)), dma((4,)), dma((4,)),
        dma((6,)), dma((6,)), dma((16,)), dma((16,)), dma((8,)), dma((8,)), dma((4,)), dma((4,)), dma((4,)), dma((4,)),
        dma((4,)), dma((4,)), dma((4, 6)), dma((4, 6)), dma((4, 4)), dma((16,)),
    ]
    vmem = pl.BlockSpec(memory_space=pltpu.VMEM)
    hbm = pl.BlockSpec(memory_space=pltpu.HBM)
    args = (hidden.T, weight.reshape(16, 2, 64, VL), labels.reshape(1, BATCH), counts)
    shapes = (
        jax.ShapeDtypeStruct((8, 256, VL), BF),
        jax.ShapeDtypeStruct((16, 512), BF),
        jax.ShapeDtypeStruct((1,), F32),
    )
    smem = pl.BlockSpec(memory_space=pltpu.SMEM)
    made = pl.pallas_call(
        kernel,
        out_shape=(v((8, 256, VL), BF), v((16, 512), BF), shapes[2]),
        in_specs=[hbm] * 4,
        out_specs=(vmem, vmem, smem),
        scratch_shapes=scratch,
        compiler_params=pltpu.CompilerParams(
            collective_id=0, has_side_effects=True, vmem_limit_bytes=50 * 1024 * 1024
        ),
        cost_estimate=pl.CostEstimate(flops=3 * 2**30, bytes_accessed=2**22, transcendentals=2**16),
    )(*(pltpu.with_memory_space_constraint(a, pltpu.HBM) for a in args))
    gw, gh, loss = pl.pallas_call(
        hand_over,
        out_shape=shapes,
        in_specs=[vmem, vmem, hbm],
        out_specs=(hbm,) * 3,
        scratch_shapes=[pltpu.SMEM((1,), F32), dma((10,))],
        compiler_params=pltpu.CompilerParams(vmem_limit_bytes=2**20),
    )(*(pltpu.with_memory_space_constraint(a, m) for a, m in zip(made, (pltpu.VMEM, pltpu.VMEM, pltpu.HBM))))
    return gw.reshape(2048, VL), gh, loss


def solution(mesh):
    in_specs = (
        P("dp", ("section", "tensor")),
        P("dp", ("section", "tensor")),
        P("dp"),
        P("dp", ("section", "tensor")),
    )
    out_specs = (P("dp", ("section", "tensor")), P(("dp", "section", "tensor"), None), P("dp"))
    return jax.shard_map(body, mesh=mesh, in_specs=in_specs, out_specs=out_specs, check_vma=False)
```

```python
import functools

import jax
import jax.numpy as jnp
from jax import lax
from jax.experimental import pallas as pl
from jax.experimental.pallas import tpu as pltpu
from jax.sharding import PartitionSpec as P

NX, NY, NZ, NC = 4, 4, 16, 2
ZL = NZ // NX
BATCH = 128
FEAT = 64
VL = 512
MESH = pl.DeviceIdType.MESH
BF = jnp.bfloat16
F32 = jnp.float32


GATHER = (
    ("x", 0, 0),
    ("y", 2, 0), ("y", 1, 0), ("y", 3, 0),  ("x", 0, 1), ("y", 2, 1), ("y", 1, 1), ("y", 3, 1),
    ("core", 2), ("core", 1), ("logits", 2), ("core", 3), ("logits", 1), ("core", 0), ("logits", 3), ("logits", 0),
    ("sum", 3), ("sum", 1),
)
REDUCE = (
    ("dot", 2), ("dot", 1), ("dot", 3), ("dot", 0), ("own", 2), ("yd", 2, 0), ("yd", 2, 1), ("own", 1), ("yd", 1, 0), ("yd", 1, 1),
    ("own", 3), ("yd", 3, 0), ("yd", 3, 1), ("own", 0), ("y", 0), ("gw", 0), ("gw", 1), ("zd", 2, 0), ("zd", 2, 1), ("relay", 0),
    ("zd", 1, 0), ("zd", 1, 1), ("zd", 3, 0), ("zd", 3, 1), ("gw", 2), ("gw", 3), ("z", 0), ("gw", 4), ("gw", 5), ("gw", 6), ("gw", 7),
)


def spread(i):
    half = (i + 1) // 2
    return NZ // 2 + (1 - 2 * lax.rem(i, 2)) * half


def kernel(
    hid_hbm, w_hbm, lab_hbm, cnt_hbm,
    gwv, gh_out, loss_out,
    wv, wt, zbuf, ht, part, bufa, bufb, rfl, rfr, cbuf, lbuf, fcol, eb, stz, sty, coef, gall,
    psend, pown, crecv, q, ya, yb, sa, sb, yl, yr, y2, rz, zrb,
    w_sem, in_sem,
    az_s, az_r, ax_s, ax_r, ct_s, ct_r, lb_s, lb_r, ay_s, ay_r, ac_s, ac_r,
    b_s, b_r, sz_s, sz_r, sy_s, sy_r, eb_s, eb_r, co_s, co_r,
    fc_s, fc_r, fy_s, fy_r, fz_s, fz_r,
):
    x = lax.axis_index("dp")
    s = lax.axis_index("section")
    y = lax.axis_index("tensor")
    z, c = s // 2, lax.rem(s, 2)
    zs, zl0 = z // ZL, lax.rem(z, ZL)
    oc = 1 - c

    def xat(k):
        return lax.rem(x + k + NX, NX)

    def yat(k):
        return lax.rem(y + k + NY, NY)

    def zat(k):
        return lax.rem(z + k + NZ, NZ)

    def to_x(k):
        return (xat(k), s, y)

    def to_y(k):
        return (x, s, yat(k))

    def to_z(zz):
        return (x, 2 * zz + c, y)

    def to_q(k):
        j = lax.rem(y * 2 + c + k, 8)
        return (x, 2 * z + lax.rem(j, 2), j // 2)

    sibling = (x, 2 * z + oc, y)
    sends = []

    def rcopy(src, dst, ss, rs, dev):
        return pltpu.make_async_remote_copy(
            src_ref=src, dst_ref=dst, send_sem=ss, recv_sem=rs, device_id=dev, device_id_type=MESH
        )

    def send(src, dst, ss, rs, dev):
        d = rcopy(src, dst, ss, rs, dev)
        d.start()
        sends.append(d)

    def play(run, schedule):
        for name, *at in schedule:
            run[name](*at)

    def recv(dst, rs):
        rcopy(dst, dst, rs, rs, sibling).wait_recv()

    w_copy = pltpu.make_async_copy(w_hbm, wv, w_sem)
    ins = [
        pltpu.make_async_copy(hid_hbm, zbuf.at[z], in_sem.at[0]),
        pltpu.make_async_copy(cnt_hbm, cbuf.at[x], in_sem.at[1]),
        pltpu.make_async_copy(lab_hbm, lbuf.at[x], in_sem.at[2]),
    ]
    for copy in ins:
        copy.start()

    barrier = pltpu.get_barrier_semaphore()

    def greet_z(i, _):
        pl.semaphore_signal(barrier, inc=1, device_id=to_z(zat(spread(i))), device_id_type=MESH)
        return 0

    lax.fori_loop(0, NZ - 1, greet_z, 0)
    for k in range(1, 8):
        pl.semaphore_signal(barrier, inc=1, device_id=to_q(k), device_id_type=MESH)
    for k in range(1, NX):
        pl.semaphore_signal(barrier, inc=1, device_id=to_x(k), device_id_type=MESH)
    w_copy.start()
    for copy in ins:
        copy.wait()
    pl.semaphore_wait(barrier, 25)

    others = pl.ds(0, NZ - 1)
    halves = [pl.ds(0, FEAT // 2), pl.ds(FEAT // 2, FEAT // 2)]

    def start_z(h):
        def start(i, _):
            k = spread(i)
            ref = zbuf.at[z, halves[h]]
            rcopy(ref, ref, az_s.at[h], az_r.at[h], to_z(zat(k))).start()
            return 0

        lax.fori_loop(0, NZ - 1, start, 0)

    start_z(0)
    start_z(1)
    for k in range(1, NX):
        send(cbuf.at[x], cbuf.at[x], ct_s.at[k], ct_r.at[k], to_x(k))
        send(lbuf.at[x], lbuf.at[x], lb_s.at[k], lb_r.at[k], to_x(k))

    w_copy.wait()

    def turn(i, _):
        rows = wv[pl.ds(2 * i, 2)].reshape(256, VL)
        wt[:, pl.ds(pl.multiple_of(i * 256, 256), 256)] = rows.T
        return 0

    lax.fori_loop(0, 8, turn, 0)
    for k in range(1, NX):
        recv(cbuf.at[xat(-k)], ct_r.at[k])
        recv(lbuf.at[xat(-k)], lb_r.at[k])
    totals = cbuf[0] + cbuf[1] + cbuf[2] + cbuf[3]
    factor = lax.rsqrt(1.0 + totals.astype(F32))
    fcol[...] = jnp.broadcast_to(factor, (BATCH, VL)).T

    def hid_x(_, h):
        ref = zbuf.at[others, halves[h]]
        recv(ref, az_r.at[h])
        for k in (2, 1, 3):
            to = xat(k)
            send(
                zbuf.at[pl.ds(ZL * to, ZL), halves[h]], ht.at[x, :, c, y, halves[h]],
                ax_s.at[h, k], ax_r.at[h, k], to_x(k),
            )
        ht[x, :, c, y, halves[h]] = zbuf[pl.ds(ZL * x, ZL), halves[h]]
        hid_y(0, h)

    def hid_y(k, h):
        r = xat(-k)
        ref = ht.at[r, :, c, y, halves[h]]
        if k:
            recv(ref, ax_r.at[h, k])
        for e in (2, 1, 3):
            send(ref, ref, ay_s.at[h, k, e], ay_r.at[h, k, e], to_y(e))

    def hid_core(k):
        r = xat(-k)
        for h in (0, 1):
            for e in (1, 3, 2):
                recv(ht.at[r, :, c, yat(-e), halves[h]], ay_r.at[h, k, e])
        send(ht.at[r, :, c], ht.at[r, :, c], ac_s.at[k], ac_r.at[k], sibling)

    def logits_of(k):
        r = xat(-k)
        recv(ht.at[r, :, oc], ac_r.at[k])

        def tile(i, _):
            rows = pl.ds(pl.multiple_of(i * 256, 256), 256)
            part[r, rows] = jnp.dot(wt[rows, :], ht[r].reshape(2048, BATCH), preferred_element_type=F32)
            return 0

        lax.fori_loop(0, 2, tile, 0)
        top, low = pl.ds(0, 256), pl.ds(256, 256)
        if k == 2:
            send(part.at[r, top], bufa, b_s.at[0], b_r.at[0], to_x(1))
            send(part.at[r, low], bufb, b_s.at[1], b_r.at[1], to_x(-1))
        if k == 3:
            send(part.at[r, low], rfl.at[low], b_s.at[2], b_r.at[2], to_x(1))
        if k == 1:
            send(part.at[r, top], rfr.at[top], b_s.at[4], b_r.at[4], to_x(-1))

    def logits_relay(k):
        r = xat(-k)
        top, low = pl.ds(0, 256), pl.ds(256, 256)
        if k == 3:
            recv(bufa, b_r.at[0])
            part[r, top] = part[r, top] + bufa[...]
            send(part.at[r, top], rfl.at[top], b_s.at[3], b_r.at[3], to_x(1))
        if k == 1:
            recv(bufb, b_r.at[1])
            part[r, low] = part[r, low] + bufb[...]
            send(part.at[r, low], rfr.at[low], b_s.at[5], b_r.at[5], to_x(-1))

    run = {"x": hid_x, "y": hid_y, "core": hid_core, "logits": logits_of, "sum": logits_relay}
    play(run, GATHER)

    top, low = pl.ds(0, 256), pl.ds(256, 256)
    recv(rfl.at[low], b_r.at[2])
    recv(rfl.at[top], b_r.at[3])
    recv(rfr.at[top], b_r.at[4])
    recv(rfr.at[low], b_r.at[5])

    logits = part[x] + rfl[...] + rfr[...]
    ids = lax.broadcasted_iota(jnp.int32, (VL, BATCH), 0) + (s * NY + y) * VL
    hit = ids == lbuf[x]
    m0 = jnp.max(logits, axis=0, keepdims=True)
    e0 = jnp.exp(logits - m0)
    eb[x] = e0.astype(BF)
    for k in (2, 1, 3):
        send(eb.at[x], eb.at[x], eb_s.at[k], eb_r.at[k], to_x(k))
    zero = jnp.zeros((4, BATCH), F32)
    stz[z] = jnp.concatenate(
        [
            m0,
            jnp.sum(e0, axis=0, keepdims=True),
            jnp.sum(jnp.where(hit, logits, 0.0), axis=0, keepdims=True),
            jnp.sum(jnp.where(hit, fcol[...], 0.0), axis=0, keepdims=True),
            zero,
        ],
        axis=0,
    )

    def combine(ref):
        v = ref[...]
        tops = v[:, 0:1, :]
        m = jnp.max(tops, axis=0)
        t = jnp.sum(v[:, 1:2, :] * jnp.exp(tops - m[None]), axis=0)
        return m, t, jnp.sum(v[:, 2:3, :], axis=0), jnp.sum(v[:, 3:4, :], axis=0)

    def start_sz(i, _):
        k = spread(i)
        rcopy(stz.at[z], stz.at[z], sz_s, sz_r, to_z(zat(k))).start()
        return 0

    lax.fori_loop(0, NZ - 1, start_sz, 0)
    for h in (0, 1):
        ref = zbuf.at[others, halves[h]]
        rcopy(ref, ref, az_s.at[h], az_r.at[h], sibling).wait_send()
    recv(stz.at[others], sz_r)
    me = y * 2 + c
    sty[me] = jnp.concatenate([*combine(stz), zero], axis=0)
    for k in range(1, 8):
        send(sty.at[me], sty.at[me], sy_s.at[k], sy_r.at[k], to_q(k))
    for k in range(1, 8):
        recv(sty.at[lax.rem(me - k + 8, 8)], sy_r.at[k])
    m, total, target, weight = combine(sty)
    scaled = weight / jnp.mean(weight)
    loss_out[0] = jnp.sum(scaled * (jnp.log(total) + m - target)) / BATCH
    coef[x] = jnp.concatenate([scaled * jnp.exp(m0 - m) / total, scaled, jnp.zeros((6, BATCH), F32)], axis=0)

    for k in (2, 1, 3):
        send(coef.at[x], coef.at[x], co_s.at[k], co_r.at[k], to_x(k))
    for k in (0, 1, 3, 2):
        r = xat(-k)
        if k:
            recv(eb.at[r], eb_r.at[k])
            recv(coef.at[r], co_r.at[k])
        v = coef[r]
        gall[:, pl.ds(pl.multiple_of(r * BATCH, BATCH), BATCH)] = (
            eb[r].astype(F32) * v[0:1] - jnp.where(ids == lbuf[r], v[1:2], 0.0)
        ).astype(BF)
    def gh_dot(k):
        zz = lax.rem(zs + k, NX)
        rows = wv[pl.ds(ZL * zz, ZL), oc].reshape(256, VL)
        psend[zz] = jnp.dot(rows, gall[...], preferred_element_type=F32).astype(BF).reshape(ZL, NY, 16, 512)
        send(psend.at[zz], crecv.at[zz], fc_s.at[k], fc_r.at[k], sibling)

    def gh_own(k):
        zz = lax.rem(zs + k, NX)
        rows = wv[pl.ds(ZL * zz, ZL), c].reshape(256, VL)
        pown[zz] = jnp.dot(rows, gall[...], preferred_element_type=F32).reshape(ZL, NY, 16, 512)
        recv(crecv.at[zz], fc_r.at[k])
        q[zz] = (pown[zz] + crecv[zz].astype(F32)).astype(BF)

    def gh_yd(k, h):
        zz = lax.rem(zs + k, NX)
        two = pl.ds(2 * h, 2)
        for e, ref in ((2, y2), (1, yl), (3, yr)):
            n = 3 * h + e - 1
            send(q.at[zz, two, yat(e)], ref.at[k, two], fy_s.at[k, n], fy_r.at[k, n], to_y(e))

    def gh_y(k):
        zz = lax.rem(zs + k, NX)
        up, down = pl.ds(0, 2), pl.ds(2, 2)
        send(q.at[zz, up, yat(2)], ya.at[k], fy_s.at[k, 0], fy_r.at[k, 0], to_y(1))
        send(q.at[zz, down, yat(2)], yb.at[k], fy_s.at[k, 1], fy_r.at[k, 1], to_y(-1))
        send(q.at[zz, down, yat(1)], yl.at[k, down], fy_s.at[k, 2], fy_r.at[k, 2], to_y(1))
        send(q.at[zz, up, yat(-1)], yr.at[k, up], fy_s.at[k, 3], fy_r.at[k, 3], to_y(-1))

    def gh_relay(k):
        zz = lax.rem(zs + k, NX)
        up, down = pl.ds(0, 2), pl.ds(2, 2)
        recv(ya.at[k], fy_r.at[k, 0])
        sa[k] = (q[zz, up, yat(1)].astype(F32) + ya[k].astype(F32)).astype(BF)
        send(sa.at[k], yl.at[k, up], fy_s.at[k, 4], fy_r.at[k, 4], to_y(1))
        recv(yb.at[k], fy_r.at[k, 1])
        sb[k] = (q[zz, down, yat(-1)].astype(F32) + yb[k].astype(F32)).astype(BF)
        send(sb.at[k], yr.at[k, down], fy_s.at[k, 5], fy_r.at[k, 5], to_y(-1))

    def gh_z(k):
        zz = lax.rem(zs + k, NX)
        up, down = pl.ds(0, 2), pl.ds(2, 2)
        recv(yl.at[k, down], fy_r.at[k, 2])
        recv(yr.at[k, up], fy_r.at[k, 3])
        recv(yl.at[k, up], fy_r.at[k, 4])
        recv(yr.at[k, down], fy_r.at[k, 5])
        rz[zz] = (q[zz, :, y].astype(F32) + yl[k].astype(F32) + yr[k].astype(F32)).astype(BF)
        for j in range(0 if k else 1, ZL):
            l = lax.rem(zl0 + j, ZL)
            send(rz.at[zz, l], zrb.at[z], fz_s.at[k, j], fz_r, to_z(ZL * zz + l))

    def gh_zd(k, h):
        zz = lax.rem(zs + k, NX)
        two = pl.ds(2 * h, 2)
        for e, ref in ((1, yl), (3, yr), (2, y2)):
            recv(ref.at[k, two], fy_r.at[k, 3 * h + e - 1])
        near = yl[k, two].astype(F32) + yr[k, two].astype(F32)
        rz[zz, two] = (q[zz, two, y].astype(F32) + near + y2[k, two].astype(F32)).astype(BF)
        for j in (2 * h, 2 * h + 1):
            send(rz.at[zz, j], zrb.at[z], fz_s.at[k, j], fz_r, to_z(ZL * zz + j))

    def gw_tile(i):
        lhs = jnp.concatenate([ht[r, i // 2, i % 2].reshape(256, BATCH) for r in range(NX)], axis=1)
        gwv[i] = lax.dot_general(lhs, gall[...], (((1,), (1,)), ((), ())), preferred_element_type=F32).astype(BF)

    run = {
        "dot": gh_dot, "own": gh_own, "y": gh_y, "yd": gh_yd, "relay": gh_relay, "z": gh_z, "zd": gh_zd, "gw": gw_tile,
    }
    play(run, REDUCE)

    zrb[z] = rz[zs, zl0]

    rcopy(stz.at[others], stz.at[others], sz_s, sz_r, sibling).wait_send()
    recv(zrb.at[others], fz_r)
    gh_out[...] = jnp.sum(zrb[...].astype(F32), axis=0).astype(BF)

    for d in sends:
        d.wait_send()


def hand_over(gw_in, gh_in, loss_in, gw_out, gh_out, loss_out, held, sem):
    copies = [pltpu.make_async_copy(gw_in.at[i], gw_out.at[i], sem.at[i]) for i in range(8)]
    copies.append(pltpu.make_async_copy(gh_in, gh_out, sem.at[8]))
    first = pltpu.make_async_copy(loss_in, held, sem.at[9])
    first.start()
    for copy in copies:
        copy.start()
    first.wait()
    copies.append(pltpu.make_async_copy(held, loss_out, sem.at[9]))
    copies[-1].start()
    for copy in copies:
        copy.wait()


def body(hidden, weight, labels, counts):
    dma = pltpu.SemaphoreType.DMA
    v = pltpu.VMEM
    scratch = [
        v((16, 2, 64, VL), BF),
        v((VL, 2048), BF),
        v((NZ, FEAT, BATCH), BF),
        v((NX, ZL, NC, NY, FEAT, BATCH), BF),
        v((NX, VL, BATCH), F32),
        v((256, BATCH), F32),
        v((256, BATCH), F32),
        v((VL, BATCH), F32),
        v((VL, BATCH), F32),
        v((NX, 1, VL), jnp.int32),
        v((NX, 1, BATCH), jnp.int32),
        v((VL, BATCH), F32),
        v((NX, VL, BATCH), BF),
        v((NZ, 8, BATCH), F32),
        v((8, 8, BATCH), F32),
        v((NX, 8, BATCH), F32),
        v((VL, NX * BATCH), BF),
        v((NX, ZL, NY, 16, 512), BF),
        v((NX, ZL, NY, 16, 512), F32),
        v((NX, ZL, NY, 16, 512), BF),
        v((NX, ZL, NY, 16, 512), BF),
        v((NX, 2, 16, 512), BF),
        v((NX, 2, 16, 512), BF),
        v((NX, 2, 16, 512), BF),
        v((NX, 2, 16, 512), BF),
        v((NX, ZL, 16, 512), BF),
        v((NX, ZL, 16, 512), BF),
        v((NX, ZL, 16, 512), BF),
        v((NX, ZL, 16, 512), BF),
        v((NZ, 16, 512), BF),
        dma, dma((3,)),
        dma((2,)), dma((2,)), dma((2, 4)), dma((2, 4)), dma((4,)), dma((4,)), dma((4,)), dma((4,)),
        dma((2, 4, 4)), dma((2, 4, 4)), dma((4,)), dma((4,)),
        dma((6,)), dma((6,)), dma, dma, dma((8,)), dma((8,)), dma((4,)), dma((4,)), dma((4,)), dma((4,)),
        dma((4,)), dma((4,)), dma((4, 6)), dma((4, 6)), dma((4, 4)), dma,
    ]
    vmem = pl.BlockSpec(memory_space=pltpu.VMEM)
    hbm = pl.BlockSpec(memory_space=pltpu.HBM)
    args = (hidden.T, weight.reshape(16, 2, 64, VL), labels.reshape(1, BATCH), counts)
    shapes = (
        jax.ShapeDtypeStruct((8, 256, VL), BF),
        jax.ShapeDtypeStruct((16, 512), BF),
        jax.ShapeDtypeStruct((1,), F32),
    )
    smem = pl.BlockSpec(memory_space=pltpu.SMEM)
    made = pl.pallas_call(
        kernel,
        out_shape=(v((8, 256, VL), BF), v((16, 512), BF), shapes[2]),
        in_specs=[hbm] * 4,
        out_specs=(vmem, vmem, smem),
        scratch_shapes=scratch,
        compiler_params=pltpu.CompilerParams(
            collective_id=0, has_side_effects=True, vmem_limit_bytes=50 * 1024 * 1024
        ),
        cost_estimate=pl.CostEstimate(flops=3 * 2**30, bytes_accessed=2**22, transcendentals=2**16),
    )(*(pltpu.with_memory_space_constraint(a, pltpu.HBM) for a in args))
    gw, gh, loss = pl.pallas_call(
        hand_over,
        out_shape=shapes,
        in_specs=[vmem, vmem, hbm],
        out_specs=(hbm,) * 3,
        scratch_shapes=[pltpu.SMEM((1,), F32), dma((10,))],
        compiler_params=pltpu.CompilerParams(vmem_limit_bytes=2**20),
    )(*(pltpu.with_memory_space_constraint(a, m) for a, m in zip(made, (pltpu.VMEM, pltpu.VMEM, pltpu.HBM))))
    return gw.reshape(2048, VL), gh, loss


def solution(mesh):
    in_specs = (
        P("dp", ("section", "tensor")),
        P("dp", ("section", "tensor")),
        P("dp"),
        P("dp", ("section", "tensor")),
    )
    out_specs = (P("dp", ("section", "tensor")), P(("dp", "section", "tensor"), None), P("dp"))
    return jax.shard_map(body, mesh=mesh, in_specs=in_specs, out_specs=out_specs, check_vma=False)
```

```python
import functools

import jax
import jax.numpy as jnp
from jax import lax
from jax.experimental import pallas as pl
from jax.experimental.pallas import tpu as pltpu
from jax.sharding import PartitionSpec as P

NX, NY, NZ, NC = 4, 4, 16, 2
ZL = NZ // NX
BATCH = 128
FEAT = 64
VL = 512
MESH = pl.DeviceIdType.MESH
BF = jnp.bfloat16
F32 = jnp.float32


GATHER = (
    ("x", 0, 0),
    ("y", 2, 0), ("y", 1, 0), ("y", 3, 0),  ("x", 0, 1), ("y", 2, 1), ("y", 1, 1), ("y", 3, 1),
    ("core", 2), ("core", 1), ("logits", 2), ("core", 3), ("logits", 1), ("core", 0), ("logits", 3), ("logits", 0),
    ("sum", 3), ("sum", 1),
)
REDUCE = (
    ("dot", 2), ("dot", 1), ("dot", 3), ("dot", 0), ("own", 2), ("yd", 2, 0), ("yd", 2, 1), ("own", 1), ("yd", 1, 0), ("yd", 1, 1),
    ("own", 3), ("yd", 3, 0), ("yd", 3, 1), ("own", 0), ("y", 0), ("gw", 0), ("gw", 1), ("zd", 2, 0), ("zd", 2, 1), ("relay", 0),
    ("zd", 1, 0), ("zd", 1, 1), ("zd", 3, 0), ("zd", 3, 1), ("gw", 2), ("gw", 3), ("z", 0), ("gw", 4), ("gw", 5), ("gw", 6), ("gw", 7),
)


def spread(i):
    half = (i + 1) // 2
    return NZ // 2 + (1 - 2 * lax.rem(i, 2)) * half


def kernel(
    hid_hbm, w_hbm, lab_hbm, cnt_hbm,
    gwv, gh_out, loss_out,
    wv, wt, zbuf, ht, part, bufa, bufb, rfl, rfr, cbuf, lbuf, fcol, eb, stz, sty, coef, gall,
    psend, pown, crecv, q, ya, yb, sa, sb, yl, yr, y2, rz, zrb,
    w_sem, in_sem,
    az_s, az_r, ax_s, ax_r, ct_s, ct_r, lb_s, lb_r, ay_s, ay_r, ac_s, ac_r,
    b_s, b_r, sz_s, sz_r, sy_s, sy_r, eb_s, eb_r, co_s, co_r,
    fc_s, fc_r, fy_s, fy_r, fz_s, fz_r,
):
    x = lax.axis_index("dp")
    s = lax.axis_index("section")
    y = lax.axis_index("tensor")
    z, c = s // 2, lax.rem(s, 2)
    zs, zl0 = z // ZL, lax.rem(z, ZL)
    oc = 1 - c

    def xat(k):
        return lax.rem(x + k + NX, NX)

    def yat(k):
        return lax.rem(y + k + NY, NY)

    def zat(k):
        return lax.rem(z + k + NZ, NZ)

    def to_x(k):
        return (xat(k), s, y)

    def to_y(k):
        return (x, s, yat(k))

    def to_z(zz):
        return (x, 2 * zz + c, y)

    def to_q(k):
        j = lax.rem(y * 2 + c + k, 8)
        return (x, 2 * z + lax.rem(j, 2), j // 2)

    sibling = (x, 2 * z + oc, y)
    sends = []

    def rcopy(src, dst, ss, rs, dev):
        return pltpu.make_async_remote_copy(
            src_ref=src, dst_ref=dst, send_sem=ss, recv_sem=rs, device_id=dev, device_id_type=MESH
        )

    def send(src, dst, ss, rs, dev):
        d = rcopy(src, dst, ss, rs, dev)
        d.start()
        sends.append(d)

    def play(run, schedule):
        for name, *at in schedule:
            run[name](*at)

    def recv(dst, rs):
        rcopy(dst, dst, rs, rs, sibling).wait_recv()

    w_copy = pltpu.make_async_copy(w_hbm, wv, w_sem)
    ins = [
        pltpu.make_async_copy(hid_hbm, zbuf.at[z], in_sem.at[0]),
        pltpu.make_async_copy(cnt_hbm, cbuf.at[x], in_sem.at[1]),
        pltpu.make_async_copy(lab_hbm, lbuf.at[x], in_sem.at[2]),
    ]
    for copy in ins:
        copy.start()

    barrier = pltpu.get_barrier_semaphore()

    def greet_z(i, _):
        pl.semaphore_signal(barrier, inc=1, device_id=to_z(zat(spread(i))), device_id_type=MESH)
        return 0

    lax.fori_loop(0, NZ - 1, greet_z, 0)
    for k in range(1, 8):
        pl.semaphore_signal(barrier, inc=1, device_id=to_q(k), device_id_type=MESH)
    for k in range(1, NX):
        pl.semaphore_signal(barrier, inc=1, device_id=to_x(k), device_id_type=MESH)
    w_copy.start()
    for copy in ins:
        copy.wait()
    pl.semaphore_wait(barrier, 25)

    others = pl.ds(0, NZ - 1)
    halves = [pl.ds(0, FEAT // 2), pl.ds(FEAT // 2, FEAT // 2)]

    def start_z(h):
        def start(i, _):
            k = spread(i)
            ref = zbuf.at[z, halves[h]]
            rcopy(ref, ref, az_s.at[h], az_r.at[h], to_z(zat(k))).start()
            return 0

        lax.fori_loop(0, NZ - 1, start, 0)

    start_z(0)
    start_z(1)
    for k in range(1, NX):
        send(cbuf.at[x], cbuf.at[x], ct_s.at[k], ct_r.at[k], to_x(k))
        send(lbuf.at[x], lbuf.at[x], lb_s.at[k], lb_r.at[k], to_x(k))

    w_copy.wait()

    def turn(i, _):
        rows = wv[pl.ds(2 * i, 2)].reshape(256, VL)
        wt[:, pl.ds(pl.multiple_of(i * 256, 256), 256)] = rows.T
        return 0

    lax.fori_loop(0, 8, turn, 0)
    for k in range(1, NX):
        recv(cbuf.at[xat(-k)], ct_r.at[k])
        recv(lbuf.at[xat(-k)], lb_r.at[k])
    totals = cbuf[0] + cbuf[1] + cbuf[2] + cbuf[3]
    factor = lax.rsqrt(1.0 + totals.astype(F32))
    fcol[...] = jnp.broadcast_to(factor, (BATCH, VL)).T

    def hid_x(_, h):
        ref = zbuf.at[others, halves[h]]
        recv(ref, az_r.at[h])
        for k in (2, 1, 3):
            to = xat(k)
            send(
                zbuf.at[pl.ds(ZL * to, ZL), halves[h]], ht.at[x, :, c, y, halves[h]],
                ax_s.at[h, k], ax_r.at[h, k], to_x(k),
            )
        ht[x, :, c, y, halves[h]] = zbuf[pl.ds(ZL * x, ZL), halves[h]]
        hid_y(0, h)

    def hid_y(k, h):
        r = xat(-k)
        ref = ht.at[r, :, c, y, halves[h]]
        if k:
            recv(ref, ax_r.at[h, k])
        for e in (2, 1, 3):
            send(ref, ref, ay_s.at[h, k, e], ay_r.at[h, k, e], to_y(e))

    def hid_core(k):
        r = xat(-k)
        for h in (0, 1):
            for e in (1, 3, 2):
                recv(ht.at[r, :, c, yat(-e), halves[h]], ay_r.at[h, k, e])
        send(ht.at[r, :, c], ht.at[r, :, c], ac_s.at[k], ac_r.at[k], sibling)

    def logits_of(k):
        r = xat(-k)
        recv(ht.at[r, :, oc], ac_r.at[k])

        top, low = pl.ds(0, 256), pl.ds(256, 256)

        def tile(rows):
            part[r, rows] = jnp.dot(wt[rows, :], ht[r].reshape(2048, BATCH), preferred_element_type=F32)

        tile(low if k == 3 else top)
        if k == 2:
            send(part.at[r, top], bufa, b_s.at[0], b_r.at[0], to_x(1))
        if k == 3:
            send(part.at[r, low], rfl.at[low], b_s.at[2], b_r.at[2], to_x(1))
        if k == 1:
            send(part.at[r, top], rfr.at[top], b_s.at[4], b_r.at[4], to_x(-1))
        tile(top if k == 3 else low)
        if k == 2:
            send(part.at[r, low], bufb, b_s.at[1], b_r.at[1], to_x(-1))
    def logits_relay(k):
        r = xat(-k)
        top, low = pl.ds(0, 256), pl.ds(256, 256)
        if k == 3:
            recv(bufa, b_r.at[0])
            part[r, top] = part[r, top] + bufa[...]
            send(part.at[r, top], rfl.at[top], b_s.at[3], b_r.at[3], to_x(1))
        if k == 1:
            recv(bufb, b_r.at[1])
            part[r, low] = part[r, low] + bufb[...]
            send(part.at[r, low], rfr.at[low], b_s.at[5], b_r.at[5], to_x(-1))

    run = {"x": hid_x, "y": hid_y, "core": hid_core, "logits": logits_of, "sum": logits_relay}
    play(run, GATHER)

    top, low = pl.ds(0, 256), pl.ds(256, 256)
    recv(rfl.at[low], b_r.at[2])
    recv(rfl.at[top], b_r.at[3])
    recv(rfr.at[top], b_r.at[4])
    recv(rfr.at[low], b_r.at[5])

    logits = part[x] + rfl[...] + rfr[...]
    ids = lax.broadcasted_iota(jnp.int32, (VL, BATCH), 0) + (s * NY + y) * VL
    hit = ids == lbuf[x]
    m0 = jnp.max(logits, axis=0, keepdims=True)
    e0 = jnp.exp(logits - m0)
    eb[x] = e0.astype(BF)
    for k in (2, 1, 3):
        send(eb.at[x], eb.at[x], eb_s.at[k], eb_r.at[k], to_x(k))
    zero = jnp.zeros((4, BATCH), F32)
    stz[z] = jnp.concatenate(
        [
            m0,
            jnp.sum(e0, axis=0, keepdims=True),
            jnp.sum(jnp.where(hit, logits, 0.0), axis=0, keepdims=True),
            jnp.sum(jnp.where(hit, fcol[...], 0.0), axis=0, keepdims=True),
            zero,
        ],
        axis=0,
    )

    def combine(ref):
        v = ref[...]
        tops = v[:, 0:1, :]
        m = jnp.max(tops, axis=0)
        t = jnp.sum(v[:, 1:2, :] * jnp.exp(tops - m[None]), axis=0)
        return m, t, jnp.sum(v[:, 2:3, :], axis=0), jnp.sum(v[:, 3:4, :], axis=0)

    def start_sz(i, _):
        k = spread(i)
        rcopy(stz.at[z], stz.at[z], sz_s, sz_r, to_z(zat(k))).start()
        return 0

    lax.fori_loop(0, NZ - 1, start_sz, 0)
    for h in (0, 1):
        ref = zbuf.at[others, halves[h]]
        rcopy(ref, ref, az_s.at[h], az_r.at[h], sibling).wait_send()
    recv(stz.at[others], sz_r)
    me = y * 2 + c
    sty[me] = jnp.concatenate([*combine(stz), zero], axis=0)
    for k in range(1, 8):
        send(sty.at[me], sty.at[me], sy_s.at[k], sy_r.at[k], to_q(k))
    for k in range(1, 8):
        recv(sty.at[lax.rem(me - k + 8, 8)], sy_r.at[k])
    m, total, target, weight = combine(sty)
    scaled = weight / jnp.mean(weight)
    loss_out[0] = jnp.sum(scaled * (jnp.log(total) + m - target)) / BATCH
    coef[x] = jnp.concatenate([scaled * jnp.exp(m0 - m) / total, scaled, jnp.zeros((6, BATCH), F32)], axis=0)

    for k in (2, 1, 3):
        send(coef.at[x], coef.at[x], co_s.at[k], co_r.at[k], to_x(k))
    for k in (0, 1, 3, 2):
        r = xat(-k)
        if k:
            recv(eb.at[r], eb_r.at[k])
            recv(coef.at[r], co_r.at[k])
        v = coef[r]
        gall[:, pl.ds(pl.multiple_of(r * BATCH, BATCH), BATCH)] = (
            eb[r].astype(F32) * v[0:1] - jnp.where(ids == lbuf[r], v[1:2], 0.0)
        ).astype(BF)
    def gh_dot(k):
        zz = lax.rem(zs + k, NX)
        rows = wv[pl.ds(ZL * zz, ZL), oc].reshape(256, VL)
        psend[zz] = jnp.dot(rows, gall[...], preferred_element_type=F32).astype(BF).reshape(ZL, NY, 16, 512)
        send(psend.at[zz], crecv.at[zz], fc_s.at[k], fc_r.at[k], sibling)

    def gh_own(k):
        zz = lax.rem(zs + k, NX)
        rows = wv[pl.ds(ZL * zz, ZL), c].reshape(256, VL)
        pown[zz] = jnp.dot(rows, gall[...], preferred_element_type=F32).reshape(ZL, NY, 16, 512)
        recv(crecv.at[zz], fc_r.at[k])
        q[zz] = (pown[zz] + crecv[zz].astype(F32)).astype(BF)

    def gh_yd(k, h):
        zz = lax.rem(zs + k, NX)
        two = pl.ds(2 * h, 2)
        for e, ref in ((2, y2), (1, yl), (3, yr)):
            n = 3 * h + e - 1
            send(q.at[zz, two, yat(e)], ref.at[k, two], fy_s.at[k, n], fy_r.at[k, n], to_y(e))

    def gh_y(k):
        zz = lax.rem(zs + k, NX)
        up, down = pl.ds(0, 2), pl.ds(2, 2)
        send(q.at[zz, up, yat(2)], ya.at[k], fy_s.at[k, 0], fy_r.at[k, 0], to_y(1))
        send(q.at[zz, down, yat(2)], yb.at[k], fy_s.at[k, 1], fy_r.at[k, 1], to_y(-1))
        send(q.at[zz, down, yat(1)], yl.at[k, down], fy_s.at[k, 2], fy_r.at[k, 2], to_y(1))
        send(q.at[zz, up, yat(-1)], yr.at[k, up], fy_s.at[k, 3], fy_r.at[k, 3], to_y(-1))

    def gh_relay(k):
        zz = lax.rem(zs + k, NX)
        up, down = pl.ds(0, 2), pl.ds(2, 2)
        recv(ya.at[k], fy_r.at[k, 0])
        sa[k] = (q[zz, up, yat(1)].astype(F32) + ya[k].astype(F32)).astype(BF)
        send(sa.at[k], yl.at[k, up], fy_s.at[k, 4], fy_r.at[k, 4], to_y(1))
        recv(yb.at[k], fy_r.at[k, 1])
        sb[k] = (q[zz, down, yat(-1)].astype(F32) + yb[k].astype(F32)).astype(BF)
        send(sb.at[k], yr.at[k, down], fy_s.at[k, 5], fy_r.at[k, 5], to_y(-1))

    def gh_z(k):
        zz = lax.rem(zs + k, NX)
        up, down = pl.ds(0, 2), pl.ds(2, 2)
        recv(yl.at[k, down], fy_r.at[k, 2])
        recv(yr.at[k, up], fy_r.at[k, 3])
        recv(yl.at[k, up], fy_r.at[k, 4])
        recv(yr.at[k, down], fy_r.at[k, 5])
        rz[zz] = (q[zz, :, y].astype(F32) + yl[k].astype(F32) + yr[k].astype(F32)).astype(BF)
        for j in range(0 if k else 1, ZL):
            l = lax.rem(zl0 + j, ZL)
            send(rz.at[zz, l], zrb.at[z], fz_s.at[k, j], fz_r, to_z(ZL * zz + l))

    def gh_zd(k, h):
        zz = lax.rem(zs + k, NX)
        two = pl.ds(2 * h, 2)
        for e, ref in ((1, yl), (3, yr), (2, y2)):
            recv(ref.at[k, two], fy_r.at[k, 3 * h + e - 1])
        near = yl[k, two].astype(F32) + yr[k, two].astype(F32)
        rz[zz, two] = (q[zz, two, y].astype(F32) + near + y2[k, two].astype(F32)).astype(BF)
        for j in (2 * h, 2 * h + 1):
            send(rz.at[zz, j], zrb.at[z], fz_s.at[k, j], fz_r, to_z(ZL * zz + j))

    def gw_tile(i):
        lhs = jnp.concatenate([ht[r, i // 2, i % 2].reshape(256, BATCH) for r in range(NX)], axis=1)
        gwv[i] = lax.dot_general(lhs, gall[...], (((1,), (1,)), ((), ())), preferred_element_type=F32).astype(BF)

    run = {
        "dot": gh_dot, "own": gh_own, "y": gh_y, "yd": gh_yd, "relay": gh_relay, "z": gh_z, "zd": gh_zd, "gw": gw_tile,
    }
    play(run, REDUCE)

    zrb[z] = rz[zs, zl0]

    rcopy(stz.at[others], stz.at[others], sz_s, sz_r, sibling).wait_send()
    recv(zrb.at[others], fz_r)
    gh_out[...] = jnp.sum(zrb[...].astype(F32), axis=0).astype(BF)

    for d in sends:
        d.wait_send()


def hand_over(gw_in, gh_in, loss_in, gw_out, gh_out, loss_out, held, sem):
    copies = [pltpu.make_async_copy(gw_in.at[i], gw_out.at[i], sem.at[i]) for i in range(8)]
    copies.append(pltpu.make_async_copy(gh_in, gh_out, sem.at[8]))
    first = pltpu.make_async_copy(loss_in, held, sem.at[9])
    first.start()
    for copy in copies:
        copy.start()
    first.wait()
    copies.append(pltpu.make_async_copy(held, loss_out, sem.at[9]))
    copies[-1].start()
    for copy in copies:
        copy.wait()


def body(hidden, weight, labels, counts):
    dma = pltpu.SemaphoreType.DMA
    v = pltpu.VMEM
    scratch = [
        v((16, 2, 64, VL), BF),
        v((VL, 2048), BF),
        v((NZ, FEAT, BATCH), BF),
        v((NX, ZL, NC, NY, FEAT, BATCH), BF),
        v((NX, VL, BATCH), F32),
        v((256, BATCH), F32),
        v((256, BATCH), F32),
        v((VL, BATCH), F32),
        v((VL, BATCH), F32),
        v((NX, 1, VL), jnp.int32),
        v((NX, 1, BATCH), jnp.int32),
        v((VL, BATCH), F32),
        v((NX, VL, BATCH), BF),
        v((NZ, 8, BATCH), F32),
        v((8, 8, BATCH), F32),
        v((NX, 8, BATCH), F32),
        v((VL, NX * BATCH), BF),
        v((NX, ZL, NY, 16, 512), BF),
        v((NX, ZL, NY, 16, 512), F32),
        v((NX, ZL, NY, 16, 512), BF),
        v((NX, ZL, NY, 16, 512), BF),
        v((NX, 2, 16, 512), BF),
        v((NX, 2, 16, 512), BF),
        v((NX, 2, 16, 512), BF),
        v((NX, 2, 16, 512), BF),
        v((NX, ZL, 16, 512), BF),
        v((NX, ZL, 16, 512), BF),
        v((NX, ZL, 16, 512), BF),
        v((NX, ZL, 16, 512), BF),
        v((NZ, 16, 512), BF),
        dma, dma((3,)),
        dma((2,)), dma((2,)), dma((2, 4)), dma((2, 4)), dma((4,)), dma((4,)), dma((4,)), dma((4,)),
        dma((2, 4, 4)), dma((2, 4, 4)), dma((4,)), dma((4,)),
        dma((6,)), dma((6,)), dma, dma, dma((8,)), dma((8,)), dma((4,)), dma((4,)), dma((4,)), dma((4,)),
        dma((4,)), dma((4,)), dma((4, 6)), dma((4, 6)), dma((4, 4)), dma,
    ]
    vmem = pl.BlockSpec(memory_space=pltpu.VMEM)
    hbm = pl.BlockSpec(memory_space=pltpu.HBM)
    args = (hidden.T, weight.reshape(16, 2, 64, VL), labels.reshape(1, BATCH), counts)
    shapes = (
        jax.ShapeDtypeStruct((8, 256, VL), BF),
        jax.ShapeDtypeStruct((16, 512), BF),
        jax.ShapeDtypeStruct((1,), F32),
    )
    smem = pl.BlockSpec(memory_space=pltpu.SMEM)
    made = pl.pallas_call(
        kernel,
        out_shape=(v((8, 256, VL), BF), v((16, 512), BF), shapes[2]),
        in_specs=[hbm] * 4,
        out_specs=(vmem, vmem, smem),
        scratch_shapes=scratch,
        compiler_params=pltpu.CompilerParams(
            collective_id=0, has_side_effects=True, vmem_limit_bytes=50 * 1024 * 1024
        ),
        cost_estimate=pl.CostEstimate(flops=3 * 2**30, bytes_accessed=2**22, transcendentals=2**16),
    )(*(pltpu.with_memory_space_constraint(a, pltpu.HBM) for a in args))
    gw, gh, loss = pl.pallas_call(
        hand_over,
        out_shape=shapes,
        in_specs=[vmem, vmem, hbm],
        out_specs=(hbm,) * 3,
        scratch_shapes=[pltpu.SMEM((1,), F32), dma((10,))],
        compiler_params=pltpu.CompilerParams(vmem_limit_bytes=2**20),
    )(*(pltpu.with_memory_space_constraint(a, m) for a, m in zip(made, (pltpu.VMEM, pltpu.VMEM, pltpu.HBM))))
    return gw.reshape(2048, VL), gh, loss


def solution(mesh):
    in_specs = (
        P("dp", ("section", "tensor")),
        P("dp", ("section", "tensor")),
        P("dp"),
        P("dp", ("section", "tensor")),
    )
    out_specs = (P("dp", ("section", "tensor")), P(("dp", "section", "tensor"), None), P("dp"))
    return jax.shard_map(body, mesh=mesh, in_specs=in_specs, out_specs=out_specs, check_vma=False)
```
